32 devices in a mesh: groups: 2 (over y), section: 4 (over z), tensor: 4 (over x, core).
Axes of the slice: x: 2, y: 2, z: 4, core: 2. Of those that a mesh axis runs over, the one named last changes fastest.
Arguments:
- prefill_q: bfloat16 [4096, 8192], P(('groups', 'section'), 'tensor'), parts along dimension 0, may hold values from -48 to 48
- kv_pool: bfloat16 [2, 4096, 1024], P(None, ('groups', 'section'), 'tensor'), parts along dimension 1, may hold values from -48 to 48
- decode_q: bfloat16 [64, 4, 8192], P(('groups', 'section'), None, 'tensor'), parts along dimension 0, may hold values from -48 to 48
- decode_kv: bfloat16 [2, 64, 4, 1024], P(None, ('groups', 'section'), None, 'tensor'), parts along dimension 1, may hold values from -48 to 48
- wo_weight: bfloat16 [8192, 8192], P('tensor', 'section'), may hold values from -0.0625 to 0.0625
- page_pair: int32 [8, 32], P('groups'), parts along dimension 0, may hold values from 0 to 3, never falling along the last dimension, each value on 1 to 16 neighbouring positions
- slot_owner: int32 [32, 1], P('groups'), parts along dimension 0, may hold values from 0 to 3, as said below
Outputs:
- prefill_ctx: bfloat16 [4096, 8192], P(('groups', 'section'), 'tensor'), parts along dimension 0
- decode_out: bfloat16 [64, 4, 8192], P('groups', None, 'section'), parts along dimension 0
The draws below stay inside these ranges and needn't reach their ends.
There are 2 independent parts, one for each index of `groups`. The reference program is written for one: setup_inputs(seed, part) draws one part's arguments, and reference() takes and returns one part's arrays. A program takes and returns all parts, laid end to end along the dimension named above; an argument that names none is the same for every part. Nothing has to cross between parts.
Inputs may be any that keep to these rules, and one draw needn't show every extreme that they name: `page_pair`: in each row, pair numbers never fall, every pair has 1 to 16 pages, and some pair has exactly 16. `slot_owner`: every section index decodes at least one pair and at most 8; some index decodes exactly 8. Of the 4 pairs prefilled on one section index (pairs s * 4 to s * 4 + 3), at most 2 go to one decoding index, and some section index gives exactly 2 to one.
All inputs are finite; a program needn't handle non-finite values.
Results may differ from the reference program's by a relative error of at most 0.012.
Values may be sent and summed in bfloat16 or wider, within the bound.
No kernel may reach another device: no remote copies, remote signals or barrier semaphores. Data moves between devices by JAX's collectives and lax.ppermute only.
A program may use at most 128 MiB of HBM per device.

```python
import math
import jax
import jax.numpy as jnp
import numpy as np
from jax import lax

D = 8192
HEADS = 64
KV_HEADS = 8
HEAD_DIM = 128
PAGE = 16
PAGES_DEV = 32
PAIRS_DEV = 4
STEPS = 4
DSLOT = 8
CAP = 2
LMAX = 16
TOK_DEV = 512
POOL_TOK = 2048
PAIRS = 16
SLOTS = 32
N_SECTION = 4


def query_block(key, lead_shape):
    base = jnp.clip(jax.random.normal(key, lead_shape + (HEADS * HEAD_DIM,), jnp.float32), -6.0, 6.0)
    return base.astype(jnp.bfloat16)


def cache_block(key, lead_shape):
    base = jnp.clip(jax.random.normal(key, (2,) + lead_shape + (KV_HEADS * HEAD_DIM,), jnp.float32), -6.0, 6.0)
    return base.astype(jnp.bfloat16)


def draw_prefill_q(key, part):
    key = jax.random.fold_in(key, 11)
    return query_block(key, (POOL_TOK,))


def draw_kv_pool(key, part):
    key = jax.random.fold_in(key, 12)
    return cache_block(key, (POOL_TOK,))


def draw_decode_q(key, part):
    key = jax.random.fold_in(key, 13)
    return query_block(key, (SLOTS, STEPS))


def draw_decode_kv(key, part):
    key = jax.random.fold_in(key, 14)
    return cache_block(key, (SLOTS, STEPS))


def draw_slot_owner(key, part):
    key = jax.random.fold_in(key, 21)
    key_order, key_rank, key_turn, key_offset = jax.random.split(key, 4)
    order = jax.random.permutation(key_order, N_SECTION).astype(jnp.int32)
    source_rank = jax.random.permutation(key_rank, N_SECTION).astype(jnp.int32)
    turn = jax.random.randint(key_turn, (N_SECTION,), 0, PAIRS_DEV, jnp.int32)
    offset = jax.random.randint(key_offset, (), 0, N_SECTION - 1, jnp.int32)
    quota = jnp.clip(DSLOT - CAP * source_rank, 0, CAP)
    local_ids = jnp.arange(PAIRS_DEV, dtype=jnp.int32)
    to_busiest = (local_ids[None, :] + turn[:, None]) % PAIRS_DEV < quota[:, None]
    flat = to_busiest.reshape(-1)
    others = 1 - flat.astype(jnp.int32)
    counter = (jnp.cumsum(others) - others).astype(jnp.int32)
    other_owner = order[1 + (counter + offset) % (N_SECTION - 1)]
    owner = jnp.where(flat, order[0], other_owner)
    return owner.reshape(PAIRS, 1).astype(jnp.int32)


def block_scale(own_key, dims, cuts, low, largest):
    factor_of, own = 1.0, jax.random.fold_in(own_key, 6)
    for position, shards_of in cuts:
        draws = jnp.exp(jax.random.uniform(jax.random.fold_in(own, position), (shards_of,), jnp.float32, low / len(cuts), largest / len(cuts)))
        factor_of = factor_of * jnp.repeat(draws, dims[position] // shards_of).reshape([-1 if axis == position else 1 for axis in range(len(dims))])
    return factor_of


def split_up(amount, total, most, lean):
    portions = [(1 << 20) // math.isqrt(standing ** lean) + 1 for standing in range(2, amount + 1)]
    spare, counts = total - most - (amount - 1), [1] * (amount - 1)
    while spare > 0:
        free = [i for i in range(amount - 1) if counts[i] < most]
        mass, remaining = sum([portions[i] for i in free]), spare
        for i in free:
            extra = min(most - counts[i], max(1, remaining * portions[i] // mass), spare)
            counts[i] = counts[i] + extra
            spare = spare - extra
    return np.array([most] + counts)


def uneven_parts(rng, number_of, total, limit, slope):
    if number_of == 2:
        one = jax.random.randint(rng, (), max(1, total - limit), min(limit, total - 1) + 1)
        return jnp.stack([one, total - one])
    sizes = jnp.asarray(split_up(number_of, total, limit, slope), jnp.int32)
    couples = (number_of - 1) // 2
    giver, sink = sizes[1:1 + 2 * couples:2], sizes[2:2 + 2 * couples:2]
    slack = jnp.minimum(giver - 1, limit - sink)
    passed = jax.random.randint(jax.random.fold_in(rng, 1), (couples,), 0, 1 << 20) % (slack + 1)
    sizes = sizes.at[1:1 + 2 * couples:2].set(giver - passed).at[2:2 + 2 * couples:2].set(sink + passed)
    return sizes[jax.random.permutation(jax.random.fold_in(rng, 2), number_of)]


def gaussian(rng, extent, scale, limit, cuts=(), held_as=jnp.bfloat16):
    entries = scale * jax.random.normal(rng, extent, jnp.float32)
    if cuts:
        entries = entries * block_scale(rng, extent, cuts, -0.22, 0.18)
    return jnp.clip(entries, -limit, limit).astype(held_as)


def setup_inputs(seed: int = 0, part: int = 0) -> dict:
    key_list = jax.random.split(jax.random.key(seed), 8)
    part_splits = jax.random.split(jax.random.fold_in(key_list[7], part), 8)
    return {
        "prefill_q": draw_prefill_q(jax.random.fold_in(jax.random.fold_in(key_list[7], part), 71), part),
        "kv_pool": draw_kv_pool(jax.random.fold_in(jax.random.fold_in(key_list[7], part), 71), part),
        "decode_q": draw_decode_q(jax.random.fold_in(jax.random.fold_in(key_list[7], part), 71), part),
        "decode_kv": draw_decode_kv(jax.random.fold_in(jax.random.fold_in(key_list[7], part), 71), part),
        "wo_weight": gaussian(key_list[4], (HEADS * HEAD_DIM, D), (HEADS * HEAD_DIM) ** -0.5, 0.0625, ((0, 4), (1, 4))),
        "page_pair": jax.vmap(lambda own: jnp.searchsorted(jnp.cumsum(uneven_parts(own, PAIRS_DEV, PAGES_DEV, LMAX, 2)), jnp.arange(PAGES_DEV), side="right"))(jax.random.split(part_splits[5], N_SECTION)).reshape((N_SECTION, PAGES_DEV)).astype(jnp.int32),
        "slot_owner": draw_slot_owner(jax.random.fold_in(jax.random.fold_in(key_list[7], part), 71), part),
    }


def pair_tables(page_pair, slot_owner):
    page_ids = jnp.arange(N_SECTION * PAGES_DEV, dtype=jnp.int32)
    page_owner_pair = (page_ids // PAGES_DEV) * PAIRS_DEV + page_pair.reshape(-1).astype(jnp.int32)
    token_pair = jnp.repeat(page_owner_pair, PAGE).astype(jnp.int32)
    owner_device = slot_owner[:, 0].astype(jnp.int32)
    pair_ids = jnp.arange(PAIRS, dtype=jnp.int32)
    same_owner = (owner_device[:, None] == owner_device[None, :]) & (pair_ids[None, :] < pair_ids[:, None])
    slot_rank = jnp.sum(same_owner.astype(jnp.int32), axis=1).astype(jnp.int32)
    slot_pair = jnp.full((SLOTS,), -1, jnp.int32).at[owner_device * DSLOT + slot_rank].set(pair_ids)
    return token_pair, slot_pair


def rounded(weights):
    return lax.optimization_barrier(weights.astype(jnp.bfloat16)).astype(jnp.float32)


def prefill_block(inputs):
    queries, cache_keys, cache_values, pair_ids = inputs
    positions = jnp.arange(TOK_DEV)
    allowed = (pair_ids[:, None] == pair_ids[None, :]) & (positions[None, :] <= positions[:, None])
    scores = jnp.einsum("tkgh,skh->kgts", queries.astype(jnp.float32), cache_keys.astype(jnp.float32)) * (HEAD_DIM ** -0.5)
    row_max = jnp.max(jnp.where(allowed, scores, -jnp.inf), axis=-1, keepdims=True)
    weights = jnp.where(allowed, jnp.exp(scores - row_max), 0.0)
    row_total = jnp.sum(weights, axis=-1)
    mixed_sum = jnp.einsum("kgts,skh->tkgh", rounded(weights), cache_values.astype(jnp.float32))
    return (mixed_sum / jnp.transpose(row_total, (2, 0, 1))[..., None]).astype(jnp.bfloat16)


def reference(prefill_q, kv_pool, decode_q, decode_kv, wo_weight, page_pair, slot_owner):
    group_size = HEADS // KV_HEADS
    token_pair, slot_pair = pair_tables(page_pair, slot_owner)
    cache_keys = kv_pool[0].reshape(POOL_TOK, KV_HEADS, HEAD_DIM)
    cache_values = kv_pool[1].reshape(POOL_TOK, KV_HEADS, HEAD_DIM)
    prefill_ctx = lax.map(prefill_block, (
        prefill_q.reshape(N_SECTION, TOK_DEV, KV_HEADS, group_size, HEAD_DIM),
        cache_keys.reshape(N_SECTION, TOK_DEV, KV_HEADS, HEAD_DIM),
        cache_values.reshape(N_SECTION, TOK_DEV, KV_HEADS, HEAD_DIM),
        token_pair.reshape(N_SECTION, TOK_DEV)))
    prefill_ctx = prefill_ctx.reshape(POOL_TOK, HEADS * HEAD_DIM)

    step_ids = jnp.arange(STEPS)
    new_allowed = (step_ids[None, :] <= step_ids[:, None]).reshape(STEPS, 1, 1, STEPS)

    def decode_slot(inputs):
        queries, new_keys, new_values, pair_id = inputs
        home_device = (jnp.maximum(pair_id, 0) // PAIRS_DEV).astype(jnp.int32)
        start_row = (home_device * TOK_DEV).astype(jnp.int32)
        slot_keys = lax.dynamic_slice_in_dim(cache_keys, start_row, TOK_DEV, 0).astype(jnp.float32)
        slot_values = lax.dynamic_slice_in_dim(cache_values, start_row, TOK_DEV, 0).astype(jnp.float32)
        key_pairs = lax.dynamic_slice_in_dim(token_pair, start_row, TOK_DEV, 0)
        cache_allowed = (key_pairs == pair_id).reshape(1, 1, 1, TOK_DEV)
        queries = queries.astype(jnp.float32)
        cache_scores = jnp.einsum("tkgh,skh->tkgs", queries, slot_keys) * (HEAD_DIM ** -0.5)
        new_scores = jnp.einsum("tkgh,ukh->tkgu", queries, new_keys.astype(jnp.float32)) * (HEAD_DIM ** -0.5)
        row_max = jnp.maximum(jnp.max(jnp.where(cache_allowed, cache_scores, -jnp.inf), axis=-1),
                              jnp.max(jnp.where(new_allowed, new_scores, -jnp.inf), axis=-1))[..., None]
        cache_w = jnp.where(cache_allowed, jnp.exp(cache_scores - row_max), 0.0)
        new_w = jnp.where(new_allowed, jnp.exp(new_scores - row_max), 0.0)
        row_total = jnp.sum(cache_w, axis=-1) + jnp.sum(new_w, axis=-1)
        mixed_sum = jnp.einsum("tkgs,skh->tkgh", rounded(cache_w), slot_values)
        mixed_sum = mixed_sum + jnp.einsum("tkgu,ukh->tkgh", rounded(new_w), new_values.astype(jnp.float32))
        context = (mixed_sum / row_total[..., None]).astype(jnp.bfloat16)
        context = jnp.where(pair_id >= 0, context, jnp.zeros_like(context))
        return context.reshape(STEPS, HEADS * HEAD_DIM)

    contexts = lax.map(decode_slot, (
        decode_q.reshape(SLOTS, STEPS, KV_HEADS, group_size, HEAD_DIM),
        decode_kv[0].reshape(SLOTS, STEPS, KV_HEADS, HEAD_DIM),
        decode_kv[1].reshape(SLOTS, STEPS, KV_HEADS, HEAD_DIM),
        slot_pair))
    decode_out = jnp.dot(contexts.reshape(SLOTS * STEPS, HEADS * HEAD_DIM), wo_weight, preferred_element_type=jnp.float32)
    decode_out = decode_out.astype(jnp.bfloat16).reshape(SLOTS, STEPS, D)
    return prefill_ctx, decode_out
```

```python
import functools

import jax
import jax.numpy as jnp
from jax import lax
from jax.experimental import pallas as pl
from jax.experimental.pallas import tpu as pltpu
from jax.sharding import PartitionSpec as P

HEAD_DIM = 128
GROUP = 8
PAGE = 16
PAIRS_DEV = 4
STEPS = 4
DSLOT = 8
TOK_DEV = 512
CAP = 2
BLOCK = 128
ROWS = PAIRS_DEV * STEPS
SCALE = HEAD_DIM ** (-0.5)
EXP2_SCALE = SCALE * 1.4426950408889634
MASKED = -1e30
VMEM_LIMIT = 48 * 1024 * 1024

SMEM_SPEC = pl.BlockSpec(memory_space=pltpu.SMEM)
VMEM_SPEC = pl.BlockSpec(memory_space=pltpu.VMEM)


def params():
    return pltpu.CompilerParams(vmem_limit_bytes=VMEM_LIMIT)


def pack_kernel(sections, where_ref, owner_ref, q_ref, kv_ref, *refs):
    outs, packed = refs[:sections], refs[sections]
    width = q_ref.shape[2]
    kv_width = kv_ref.shape[3]
    here = where_ref[0]

    def place(pair, carry):
        slot, rank = carry
        rank = jnp.where(pair % PAIRS_DEV == 0, 0, rank)
        mine = owner_ref[pair] == here

        @pl.when(mine)
        def _():
            to = (pair // PAIRS_DEV) ^ here
            packed[to, rank, :, :width] = q_ref[slot]
            packed[to, rank, :, width : width + kv_width] = kv_ref[0, slot]
            packed[to, rank, :, width + kv_width :] = kv_ref[1, slot]

        step = mine.astype(jnp.int32)
        return slot + step, rank + step

    packed[...] = jnp.zeros_like(packed)
    lax.fori_loop(0, owner_ref.shape[0], place, (jnp.int32(0), jnp.int32(0)))
    for k in range(sections):
        outs[k][...] = packed[k]


def pack(where, owner, decode_q, decode_kv, sections):
    width = decode_q.shape[2] + 2 * decode_kv.shape[3]
    block = (CAP, STEPS, width)
    return pl.pallas_call(
        functools.partial(pack_kernel, sections),
        out_shape=[jax.ShapeDtypeStruct(block, jnp.bfloat16)] * sections,
        in_specs=[SMEM_SPEC, SMEM_SPEC, VMEM_SPEC, VMEM_SPEC],
        out_specs=[VMEM_SPEC] * sections,
        scratch_shapes=[pltpu.VMEM((sections,) + block, jnp.bfloat16)],
        compiler_params=params(),
        name="pack_queries",
    )(where, owner, decode_q, decode_kv)


def prefill_kernel(heads_step, where_ref, page_ref, q_ref, k_ref, v_ref, o_ref, bias, keys, values):
    step = pl.program_id(0)
    blocks = TOK_DEV // BLOCK
    reach = 2

    @pl.when(step == 0)
    def _():
        here = where_ref[0]
        starts = pair_starts(page_ref, here)
        for i in range(blocks):
            low = max(0, i - reach) * BLOCK
            width = (i + 1) * BLOCK - low
            row = lax.broadcasted_iota(jnp.int32, (BLOCK, width), 0) + i * BLOCK
            col = lax.broadcasted_iota(jnp.int32, (BLOCK, width), 1) + low
            first = jnp.zeros((BLOCK, width), jnp.int32)
            for j in range(1, PAIRS_DEV):
                first = jnp.where(row >= starts[j], starts[j], first)
            bias[i, :, :width] = jnp.where((col <= row) & (col >= first), 0.0, MASKED)

    @pl.when(step % (GROUP // heads_step) == 0)
    def _():
        keys[...] = k_ref[0].astype(jnp.float32).T.astype(jnp.bfloat16)
        values[:, :HEAD_DIM] = v_ref[0]
        values[:, HEAD_DIM:] = jnp.ones((TOK_DEV, HEAD_DIM), jnp.bfloat16)

    for h in range(heads_step):
        cols = slice(h * HEAD_DIM, (h + 1) * HEAD_DIM)
        for i in range(blocks):
            low = max(0, i - reach) * BLOCK
            high = (i + 1) * BLOCK
            rows = slice(i * BLOCK, high)
            s = jnp.dot(q_ref[rows, cols], keys[:, low:high], preferred_element_type=jnp.float32)
            s = s + bias[i, :, : high - low]
            m = jnp.max(s, axis=1, keepdims=True)
            p = jnp.exp2((s - m) * EXP2_SCALE).astype(jnp.bfloat16)
            o = jnp.dot(p, values[low:high, :], preferred_element_type=jnp.float32)
            o_ref[rows, cols] = (o[:, :HEAD_DIM] / o[:, HEAD_DIM:]).astype(jnp.bfloat16)


def pair_starts(page_ref, here):
    starts = []
    for j in range(PAIRS_DEV):
        total = jnp.int32(0)
        for g in range(TOK_DEV // PAGE):
            total = total + (page_ref[here, g] < j).astype(jnp.int32)
        starts.append(total * PAGE)
    return starts


def prefill(where, page_pair, prefill_q, kv_pool, heads_step=2):
    heads = prefill_q.shape[1] // HEAD_DIM
    per_key = GROUP // heads_step
    return pl.pallas_call(
        functools.partial(prefill_kernel, heads_step),
        out_shape=jax.ShapeDtypeStruct(prefill_q.shape, jnp.bfloat16),
        grid=(heads // heads_step,),
        in_specs=[
            SMEM_SPEC,
            SMEM_SPEC,
            pl.BlockSpec((TOK_DEV, heads_step * HEAD_DIM), lambda h: (0, h)),
            pl.BlockSpec((1, TOK_DEV, HEAD_DIM), lambda h: (0, 0, h // per_key)),
            pl.BlockSpec((1, TOK_DEV, HEAD_DIM), lambda h: (1, 0, h // per_key)),
        ],
        out_specs=pl.BlockSpec((TOK_DEV, heads_step * HEAD_DIM), lambda h: (0, h)),
        scratch_shapes=[
            pltpu.VMEM((TOK_DEV // BLOCK, BLOCK, 3 * BLOCK), jnp.float32),
            pltpu.VMEM((HEAD_DIM, TOK_DEV), jnp.bfloat16),
            pltpu.VMEM((TOK_DEV, 2 * HEAD_DIM), jnp.bfloat16),
        ],
        compiler_params=params(),
        cost_estimate=pl.CostEstimate(
            flops=heads * TOK_DEV * TOK_DEV * HEAD_DIM * 4,
            bytes_accessed=prefill_q.size * 4 + kv_pool.size * 2,
            transcendentals=heads * TOK_DEV * TOK_DEV,
        ),
        name="prefill_attention",
    )(where, page_pair, prefill_q, kv_pool, kv_pool)


def decode_kernel(sections, where_ref, owner_ref, page_ref, kv_ref, *refs):
    got, ctx_ref, blocks, rows = refs[:sections], refs[sections], refs[sections + 1], refs[sections + 2]
    here = where_ref[0]
    kv_local = kv_ref.shape[2] // HEAD_DIM
    width = kv_local * GROUP * HEAD_DIM
    starts = pair_starts(page_ref, here) + [jnp.int32(TOK_DEV)]
    for k in range(sections):
        blocks[k] = got[k][...]
    owners = [owner_ref[here * PAIRS_DEV + j] for j in range(PAIRS_DEV)]
    for j in range(PAIRS_DEV):
        rank = jnp.int32(0)
        for i in range(j):
            rank = rank + (owners[i] == owners[j]).astype(jnp.int32)
        rows[j * STEPS : (j + 1) * STEPS, :] = blocks[owners[j] ^ here, rank].astype(jnp.float32)
    all_rows = rows[...].astype(jnp.bfloat16)

    many = GROUP * ROWS
    row = lax.broadcasted_iota(jnp.int32, (many, TOK_DEV), 0) % ROWS
    col = lax.broadcasted_iota(jnp.int32, (many, TOK_DEV), 1)
    first = jnp.full((many, TOK_DEV), starts[0], jnp.int32)
    last = jnp.full((many, TOK_DEV), starts[1], jnp.int32)
    for j in range(1, PAIRS_DEV):
        first = jnp.where(row >= j * STEPS, starts[j], first)
        last = jnp.where(row >= j * STEPS, starts[j + 1], last)
    allowed = (col >= first) & (col < last)
    new_row = lax.broadcasted_iota(jnp.int32, (many, ROWS), 0) % ROWS
    new_col = lax.broadcasted_iota(jnp.int32, (many, ROWS), 1)
    new_allowed = (new_row // STEPS == new_col // STEPS) & (new_col <= new_row)
    contract = (((1,), (1,)), ((), ()))
    for k in range(kv_local):
        q = jnp.concatenate(
            [all_rows[:, (k * GROUP + g) * HEAD_DIM : (k * GROUP + g + 1) * HEAD_DIM] for g in range(GROUP)], axis=0
        )
        cols = slice(k * HEAD_DIM, (k + 1) * HEAD_DIM)
        new_keys = all_rows[:, width + k * HEAD_DIM : width + (k + 1) * HEAD_DIM]
        at = width + (kv_local + k) * HEAD_DIM
        new_values = all_rows[:, at : at + HEAD_DIM]
        s = lax.dot_general(q, kv_ref[0, :, cols], contract, preferred_element_type=jnp.float32)
        s = jnp.where(allowed, s, MASKED)
        s_new = lax.dot_general(q, new_keys, contract, preferred_element_type=jnp.float32)
        s_new = jnp.where(new_allowed, s_new, MASKED)
        m = jnp.maximum(jnp.max(s, axis=1, keepdims=True), jnp.max(s_new, axis=1, keepdims=True))
        p = jnp.exp2((s - m) * EXP2_SCALE)
        p_new = jnp.exp2((s_new - m) * EXP2_SCALE)
        total = jnp.sum(p, axis=1, keepdims=True) + jnp.sum(p_new, axis=1, keepdims=True)
        o = jnp.dot(p.astype(jnp.bfloat16), kv_ref[1, :, cols], preferred_element_type=jnp.float32)
        o = o + jnp.dot(p_new.astype(jnp.bfloat16), new_values, preferred_element_type=jnp.float32)
        o = (o / total).astype(jnp.bfloat16)
        for g in range(GROUP):
            ctx_ref[:, (k * GROUP + g) * HEAD_DIM : (k * GROUP + g + 1) * HEAD_DIM] = o[g * ROWS : (g + 1) * ROWS]


def decode(where, owner, page_pair, kv_pool, got, sections):
    block = got[0].shape
    width = kv_pool.shape[2] * GROUP
    return pl.pallas_call(
        functools.partial(decode_kernel, sections),
        out_shape=jax.ShapeDtypeStruct((ROWS, width), jnp.bfloat16),
        in_specs=[SMEM_SPEC, SMEM_SPEC, SMEM_SPEC] + [VMEM_SPEC] * (1 + sections),
        out_specs=VMEM_SPEC,
        scratch_shapes=[
            pltpu.VMEM((sections,) + block, jnp.bfloat16),
            pltpu.VMEM((ROWS, block[2]), jnp.float32),
        ],
        compiler_params=params(),
        name="decode_attention",
    )(where, owner, page_pair, kv_pool, *got)


def project_kernel(sections, half_ref, *refs):
    ctxs, wo_ref, out_ref = refs[:sections], refs[sections], refs[sections + 1]
    del half_ref
    x = jnp.concatenate([c[...] for c in ctxs], axis=0)
    y = jnp.dot(x, wo_ref[...], preferred_element_type=jnp.float32)
    out_ref[...] = y.astype(out_ref.dtype)


def project(half, ctxs, wo, sections, dtype):
    depth, features = wo.shape
    rows = sections * ROWS
    chunk = min(256, features // 2)
    steps = features // 2 // chunk
    return pl.pallas_call(
        functools.partial(project_kernel, sections),
        out_shape=jax.ShapeDtypeStruct((rows, features // 2), dtype),
        grid_spec=pltpu.PrefetchScalarGridSpec(
            num_scalar_prefetch=1,
            grid=(steps,),
            in_specs=[pl.BlockSpec((ROWS, depth), lambda j, half: (0, 0))] * sections
            + [pl.BlockSpec((depth, chunk), lambda j, half: (0, half[0] * steps + j))],
            out_specs=pl.BlockSpec((rows, chunk), lambda j, half: (0, j)),
        ),
        compiler_params=params(),
        cost_estimate=pl.CostEstimate(
            flops=rows * depth * features, bytes_accessed=depth * features, transcendentals=0
        ),
        name="project_half",
    )(half, *ctxs, wo)


def scatter_kernel(sections, where_ref, owner_ref, mine_ref, other_ref, out_ref, table, rows):
    here, half = where_ref[0], where_ref[1]
    pairs = owner_ref.shape[0]
    slots = out_ref.shape[0]
    wide = mine_ref.shape[1]

    def clear(i, _):
        table[i] = -1
        return 0

    lax.fori_loop(0, slots, clear, 0)

    def clear_count(i, _):
        table[slots + i] = 0
        return 0

    lax.fori_loop(0, sections, clear_count, 0)

    def enter(pair, _):
        to = owner_ref[pair]
        rank = table[slots + to]
        table[to * DSLOT + rank] = pair
        table[slots + to] = rank + 1
        return 0

    lax.fori_loop(0, pairs, enter, 0)

    def halves(first, second):
        for p in range(pairs):
            rows[p, :, :wide] = first[p * STEPS : (p + 1) * STEPS, :]
            rows[p, :, wide:] = second[p * STEPS : (p + 1) * STEPS, :]

    @pl.when(half == 0)
    def _():
        halves(mine_ref, other_ref)

    @pl.when(half == 1)
    def _():
        halves(other_ref, mine_ref)

    def write(slot, _):
        pair = table[slot]

        @pl.when(pair >= 0)
        def _():
            at = ((pair // PAIRS_DEV) ^ here) * PAIRS_DEV + pair % PAIRS_DEV
            out_ref[slot] = rows[at]

        @pl.when(pair < 0)
        def _():
            out_ref[slot] = jnp.zeros(out_ref.shape[1:], out_ref.dtype)

        return 0

    lax.fori_loop(0, slots, write, 0)


def scatter(where, owner, mine, other, sections):
    slots = sections * DSLOT
    features = 2 * mine.shape[1]
    return pl.pallas_call(
        functools.partial(scatter_kernel, sections),
        out_shape=jax.ShapeDtypeStruct((slots, STEPS, features), jnp.bfloat16),
        in_specs=[SMEM_SPEC, SMEM_SPEC, VMEM_SPEC, VMEM_SPEC],
        out_specs=VMEM_SPEC,
        scratch_shapes=[
            pltpu.SMEM((slots + sections,), jnp.int32),
            pltpu.VMEM((owner.shape[0], STEPS, features), jnp.bfloat16),
        ],
        compiler_params=params(),
        name="scatter_slots",
    )(where, owner, mine, other)


def swap(x, axis, k):
    count = lax.axis_size(axis)
    return lax.ppermute(x, axis, [(i, i ^ k) for i in range(count)])


def per_device(prefill_q, kv_pool, decode_q, decode_kv, wo_weight, page_pair, slot_owner):
    sections = lax.axis_size("section")
    here = lax.axis_index("section")
    half = lax.axis_index("tensor") % 2
    where = jnp.stack([here, half]).astype(jnp.int32)
    owner = slot_owner.reshape(-1)

    packed = pack(where, owner, decode_q, decode_kv, sections)
    got = [packed[0]] + [swap(packed[k], "section", k) for k in range(1, sections)]
    prefill_ctx = prefill(where, page_pair, prefill_q, kv_pool)
    ctx = decode(where, owner, page_pair, kv_pool, got, sections)
    ctxs = [ctx] + [swap(ctx, "section", k) for k in range(1, sections)]

    away = project((1 - where[1:2]), ctxs, wo_weight, sections, jnp.bfloat16)
    came = swap(away, "tensor", 1)
    keep = project(where[1:2], ctxs, wo_weight, sections, jnp.float32)
    chip = keep + came.astype(jnp.float32)
    k = 2
    while k < lax.axis_size("tensor"):
        far = swap(chip.astype(jnp.bfloat16), "tensor", k)
        chip = chip + far.astype(jnp.float32)
        k *= 2
    mine = chip.astype(jnp.bfloat16)
    other = swap(mine, "tensor", 1)
    decode_out = scatter(where, owner, mine, other, sections)
    return (prefill_ctx, decode_out)


def solution(mesh):
    placed = (
        P(("groups", "section"), "tensor"),
        P(None, ("groups", "section"), "tensor"),
        P(("groups", "section"), None, "tensor"),
        P(None, ("groups", "section"), None, "tensor"),
        P("tensor", "section"),
        P("groups", None),
        P("groups", None),
    )
    return jax.shard_map(
        per_device,
        mesh=mesh,
        in_specs=placed,
        out_specs=(P(("groups", "section"), "tensor"), P("groups", None, "section")),
        check_vma=False,
    )
```

```python
import functools

import jax
import jax.numpy as jnp
from jax import lax
from jax.experimental import pallas as pl
from jax.experimental.pallas import tpu as pltpu
from jax.sharding import PartitionSpec as P

HEAD_DIM = 128
GROUP = 8
PAGE = 16
PAIRS_DEV = 4
STEPS = 4
DSLOT = 8
TOK_DEV = 512
CAP = 2
BLOCK = 128
ROWS = PAIRS_DEV * STEPS
SCALE = HEAD_DIM ** (-0.5)
EXP2_SCALE = SCALE * 1.4426950408889634
MASKED = -1e30
VMEM_LIMIT = 20 * 1024 * 1024
REACH = 2
LATEST = (REACH + 1) * BLOCK

SMEM_SPEC = pl.BlockSpec(memory_space=pltpu.SMEM)
VMEM_SPEC = pl.BlockSpec(memory_space=pltpu.VMEM)
ANY_SPEC = pl.BlockSpec(memory_space=pl.ANY)


def params():
    return pltpu.CompilerParams(vmem_limit_bytes=VMEM_LIMIT)


def in_hbm(x):
    return pltpu.with_memory_space_constraint(x, pltpu.HBM)


def pack_kernel(sections, owner_hbm, q_hbm, kv_hbm, *refs):
    outs = refs[:sections]
    owner, q, kv, packed, sems = refs[sections:]
    copies = [
        pltpu.make_async_copy(owner_hbm, owner, sems.at[0]),
        pltpu.make_async_copy(q_hbm, q, sems.at[1]),
        pltpu.make_async_copy(kv_hbm, kv, sems.at[2]),
    ]
    for copy in copies:
        copy.start()
    here = lax.axis_index("section")
    width, kv_width = q.shape[2], kv.shape[3]
    packed[...] = jnp.zeros_like(packed)
    for copy in copies:
        copy.wait()

    def place(pair, carry):
        slot, rank = carry
        rank = jnp.where(pair % PAIRS_DEV == 0, 0, rank)
        mine = owner[pair] == here

        @pl.when(mine)
        def _():
            to = (pair // PAIRS_DEV) ^ here
            packed[to, rank, :, :width] = q[slot]
            packed[to, rank, :, width : width + kv_width] = kv[0, slot]
            packed[to, rank, :, width + kv_width :] = kv[1, slot]

        step = mine.astype(jnp.int32)
        return slot + step, rank + step

    lax.fori_loop(0, owner.shape[0], place, (jnp.int32(0), jnp.int32(0)))
    for k in range(sections):
        outs[k][...] = packed[k]


def pack(owner, decode_q, decode_kv, sections):
    width = decode_q.shape[2] + 2 * decode_kv.shape[3]
    block = (CAP, STEPS, width)
    return pl.pallas_call(
        functools.partial(pack_kernel, sections),
        out_shape=[jax.ShapeDtypeStruct(block, jnp.bfloat16)] * sections,
        in_specs=[ANY_SPEC] * 3,
        out_specs=[VMEM_SPEC] * sections,
        scratch_shapes=[
            pltpu.SMEM(owner.shape, jnp.int32),
            pltpu.VMEM(decode_q.shape, jnp.bfloat16),
            pltpu.VMEM(decode_kv.shape, jnp.bfloat16),
            pltpu.VMEM((sections,) + block, jnp.bfloat16),
            pltpu.SemaphoreType.DMA((3,)),
        ],
        compiler_params=params(),
        name="pack_queries",
    )(in_hbm(owner), in_hbm(decode_q), in_hbm(decode_kv))


def pair_starts(page, here):
    rows = lax.broadcasted_iota(jnp.int32, page.shape, 0)
    starts = [jnp.zeros((1, 1), jnp.int32)]
    for j in range(1, PAIRS_DEV):
        lower = jnp.where((rows == here) & (page[...] < j), 1, 0)
        starts.append(jnp.sum(jnp.sum(lower, axis=1, keepdims=True), axis=0, keepdims=True) * PAGE)
    return starts + [jnp.full((1, 1), TOK_DEV, jnp.int32)]


def prefill_masks(starts, bias):
    for i in range(TOK_DEV // BLOCK):
        low = max(0, i - REACH) * BLOCK
        width = (i + 1) * BLOCK - low
        row = lax.broadcasted_iota(jnp.int32, (BLOCK, 1), 0) + i * BLOCK
        first = jnp.zeros((BLOCK, 1), jnp.int32)
        for j in range(1, PAIRS_DEV):
            first = jnp.where(row >= starts[j], starts[j], first)
        row = lax.broadcasted_iota(jnp.int32, (BLOCK, width), 0) + i * BLOCK
        col = lax.broadcasted_iota(jnp.int32, (BLOCK, width), 1) + low
        bias[i, :, :width] = jnp.where((col <= row) & (col >= first), 0.0, MASKED)


def decode_masks(starts, bias):
    row = lax.broadcasted_iota(jnp.int32, (ROWS, 1), 0) // STEPS
    first, last = jnp.zeros((ROWS, 1), jnp.int32), jnp.zeros((ROWS, 1), jnp.int32)
    for j in range(PAIRS_DEV):
        first = jnp.where(row == j, starts[j], first)
        last = jnp.where(row == j, starts[j + 1], last)
    col = lax.broadcasted_iota(jnp.int32, bias.shape, 1)
    bias[...] = jnp.where((col >= first) & (col < last), 0.0, MASKED)


def owner_tables(owner, here, pick, spread):
    pairs = owner.shape[1]
    down = lax.broadcasted_iota(jnp.int32, (pairs, pairs), 0)
    along = lax.broadcasted_iota(jnp.int32, (pairs, pairs), 1)
    owner_along = jnp.broadcast_to(owner[...], (pairs, pairs))
    owner_down = jnp.sum(jnp.where(down == along, owner_along, 0), axis=1, keepdims=True)
    same = owner_along == owner_down
    slot_rank = jnp.sum(jnp.where(same & (down < along), 1, 0), axis=0, keepdims=True)
    slot = owner[...] * DSLOT + slot_rank

    at_home = down // PAIRS_DEV == along // PAIRS_DEV
    home_rank = jnp.sum(jnp.where(same & at_home & (along < down), 1, 0), axis=1, keepdims=True)
    base = ((owner_down ^ here) * CAP + home_rank) * STEPS
    row = lax.broadcasted_iota(jnp.int32, pick.shape, 0)
    col = lax.broadcasted_iota(jnp.int32, pick.shape, 1)
    pair = lax.broadcasted_iota(jnp.int32, (pairs, 1), 0)
    at = row % STEPS
    for j in range(PAIRS_DEV):
        mine = jnp.sum(jnp.where(pair == here * PAIRS_DEV + j, base, 0), axis=0, keepdims=True)
        at = at + jnp.where(row // STEPS == j, mine, 0)
    pick[...] = (col == at).astype(jnp.float32).astype(pick.dtype)

    wide = spread.shape[1]
    pair = lax.broadcasted_iota(jnp.int32, (pairs, wide), 0)
    place = lax.broadcasted_iota(jnp.int32, (pairs, wide), 1) // STEPS
    holds = place == ((pair // PAIRS_DEV) ^ here) * PAIRS_DEV + pair % PAIRS_DEV
    slot_down = jnp.sum(jnp.where(down == along, jnp.broadcast_to(slot, (pairs, pairs)), 0), axis=1, keepdims=True)
    slot_of_place = jnp.sum(jnp.where(holds, slot_down, 0), axis=0, keepdims=True)
    row = lax.broadcasted_iota(jnp.int32, spread.shape, 0)
    col = lax.broadcasted_iota(jnp.int32, spread.shape, 1)
    spread[...] = (row == slot_of_place * STEPS + col % STEPS).astype(jnp.float32).astype(spread.dtype)


def region(ref, unit):
    k, i = unit
    wide = GROUP * HEAD_DIM
    return ref.at[pl.ds(i * BLOCK, BLOCK), pl.ds(k * wide, wide)]


def attend(unit, q, bias, keys, values, o):
    k, i = unit
    low, high = max(0, i - REACH) * BLOCK, (i + 1) * BLOCK
    width = high - low
    rows = jnp.concatenate([q[:, g * HEAD_DIM : (g + 1) * HEAD_DIM] for g in range(GROUP)], axis=0)
    s = jnp.dot(rows, keys[k, :, low:high], preferred_element_type=jnp.float32)
    s = (s.reshape(GROUP, BLOCK, width) + bias[i, :, :width][None]).reshape(GROUP * BLOCK, width)
    m = jnp.max(s, axis=1, keepdims=True)
    p = jnp.exp2((s - m) * EXP2_SCALE).astype(jnp.bfloat16)
    y = jnp.dot(p, values[k, low:high, :], preferred_element_type=jnp.float32)
    y = (y[:, :HEAD_DIM] / y[:, HEAD_DIM:]).astype(jnp.bfloat16)
    for g in range(GROUP):
        o[:, g * HEAD_DIM : (g + 1) * HEAD_DIM] = y[g * BLOCK : (g + 1) * BLOCK]


def half_columns(ref, flip):
    wide = ref.shape[-1] // 2
    half = lax.axis_index("tensor") % 2
    half = 1 - half if flip else half
    return ref.at[(slice(None),) * (len(ref.shape) - 1) + (pl.ds(pl.multiple_of(half * wide, wide), wide),)]


def flushes(units, blocks, ctx_hbm, sems):
    return [pltpu.make_async_copy(blocks.at[n], region(ctx_hbm, u), sems.at[n]) for n, u in enumerate(units)]


def first_kernel(
    units, later, page_hbm, owner_hbm, q_hbm, kv_hbm, wo_hbm, after,
    o, q_later, bias, keys, values, seen, pick, spread, wo_away,
    page, owner, kv, q, q_sems, late_sems, sems,
):
    del after
    small = [
        pltpu.make_async_copy(page_hbm, page, sems.at[0]),
        pltpu.make_async_copy(owner_hbm, owner, sems.at[1]),
    ]
    cache = pltpu.make_async_copy(kv_hbm, kv, sems.at[2])
    soon = [pltpu.make_async_copy(region(q_hbm, u), q.at[n], q_sems.at[n]) for n, u in enumerate(units)]
    late = [pltpu.make_async_copy(region(q_hbm, u), q_later.at[n], late_sems.at[n]) for n, u in enumerate(later)]
    weights = pltpu.make_async_copy(half_columns(wo_hbm, True), wo_away, sems.at[3])
    for copy in small + [cache] + soon + [weights] + late:
        copy.start()
    here = lax.axis_index("section")
    for copy in small:
        copy.wait()
    starts = pair_starts(page, here)
    prefill_masks(starts, bias)
    decode_masks(starts, seen)
    owner_tables(owner, here, pick, spread)
    cache.wait()
    for k in range(keys.shape[0]):
        cols = slice(k * HEAD_DIM, (k + 1) * HEAD_DIM)
        keys[k] = kv[0, :, cols].astype(jnp.float32).T.astype(jnp.bfloat16)
        values[k, :, :HEAD_DIM] = kv[1, :, cols]
        values[k, :, HEAD_DIM:] = jnp.ones((TOK_DEV, HEAD_DIM), jnp.bfloat16)
    for n, unit in enumerate(units):
        soon[n].wait()
        attend(unit, q.at[n], bias, keys, values, o.at[n])
    for copy in late + [weights]:
        copy.wait()


def second_kernel(units, done, q, bias, keys, values, done_o, wo_hbm, after, ctx_hbm, o, wo_keep, sems, wo_sem):
    del after
    copies = flushes(done, done_o, ctx_hbm, sems)
    copies.append(pltpu.make_async_copy(half_columns(wo_hbm, False), wo_keep, wo_sem))
    for copy in copies:
        copy.start()
    for n, unit in enumerate(units):
        attend(unit, q.at[n], bias, keys, values, o.at[n])
    for copy in copies:
        copy.wait()


def third_kernel(units, offset, done, q, bias, keys, values, done_o, ctx_in, chip_in, ctx_hbm, o, chip, sems):
    del ctx_in, chip_in, chip
    copies = flushes(done, done_o, ctx_hbm, sems)
    for copy in copies:
        copy.start()
    for n, unit in enumerate(units):
        attend(unit, q.at[offset + n], bias, keys, values, o.at[n])
    for copy in copies:
        copy.wait()


def unit_cost(units):
    pairs = sum(min(i + 1, REACH + 1) for _, i in units) * GROUP * BLOCK * BLOCK
    return pl.CostEstimate(
        flops=pairs * HEAD_DIM * 8, bytes_accessed=len(units) * BLOCK * GROUP * HEAD_DIM * 4, transcendentals=pairs
    )


def block_shape(units):
    return jax.ShapeDtypeStruct((len(units), BLOCK, GROUP * HEAD_DIM), jnp.bfloat16)


def prefill_first(units, later, page_pair, owner, prefill_q, kv_pool, wo, after, sections):
    kv_local = kv_pool.shape[2] // HEAD_DIM
    return pl.pallas_call(
        functools.partial(first_kernel, units, later),
        out_shape=[
            block_shape(units),
            block_shape(later),
            jax.ShapeDtypeStruct((TOK_DEV // BLOCK, BLOCK, LATEST), jnp.float32),
            jax.ShapeDtypeStruct((kv_local, HEAD_DIM, TOK_DEV), jnp.bfloat16),
            jax.ShapeDtypeStruct((kv_local, TOK_DEV, 2 * HEAD_DIM), jnp.bfloat16),
            jax.ShapeDtypeStruct((ROWS, TOK_DEV), jnp.float32),
            jax.ShapeDtypeStruct((ROWS, sections * CAP * STEPS), jnp.bfloat16),
            jax.ShapeDtypeStruct((sections * DSLOT * STEPS, sections * ROWS), jnp.bfloat16),
            jax.ShapeDtypeStruct((wo.shape[0], wo.shape[1] // 2), wo.dtype),
        ],
        in_specs=[ANY_SPEC] * 6,
        out_specs=[VMEM_SPEC] * 9,
        scratch_shapes=[
            pltpu.VMEM(page_pair.shape, jnp.int32),
            pltpu.VMEM(owner.shape, jnp.int32),
            pltpu.VMEM(kv_pool.shape, jnp.bfloat16),
            pltpu.VMEM(block_shape(units).shape, jnp.bfloat16),
            pltpu.SemaphoreType.DMA((len(units),)),
            pltpu.SemaphoreType.DMA((len(later),)),
            pltpu.SemaphoreType.DMA((4,)),
        ],
        compiler_params=params(),
        cost_estimate=unit_cost(units),
        name="prefill_first",
    )(in_hbm(page_pair), in_hbm(owner), in_hbm(prefill_q), in_hbm(kv_pool), in_hbm(wo), after)


def prefill_second(units, done, q, tables, done_o, wo, ctx_shape, after):
    return pl.pallas_call(
        functools.partial(second_kernel, units, done),
        out_shape=[
            ctx_shape,
            block_shape(units),
            jax.ShapeDtypeStruct((wo.shape[0], wo.shape[1] // 2), wo.dtype),
        ],
        in_specs=[VMEM_SPEC] * 5 + [ANY_SPEC] * 2,
        out_specs=[ANY_SPEC, VMEM_SPEC, VMEM_SPEC],
        scratch_shapes=[pltpu.SemaphoreType.DMA((len(done),)), pltpu.SemaphoreType.DMA],
        compiler_params=params(),
        cost_estimate=unit_cost(units),
        name="prefill_second",
    )(q, *tables, done_o, in_hbm(wo), after)


def prefill_third(units, offset, done, q, tables, done_o, ctx, chip):
    return pl.pallas_call(
        functools.partial(third_kernel, units, offset, done),
        out_shape=[
            jax.ShapeDtypeStruct(ctx.shape, ctx.dtype),
            block_shape(units),
            jax.ShapeDtypeStruct(chip.shape, chip.dtype),
        ],
        in_specs=[VMEM_SPEC] * 5 + [ANY_SPEC, VMEM_SPEC],
        out_specs=[ANY_SPEC, VMEM_SPEC, VMEM_SPEC],
        scratch_shapes=[pltpu.SemaphoreType.DMA((len(done),))],
        input_output_aliases={5: 0, 6: 2},
        compiler_params=params(),
        cost_estimate=unit_cost(units),
        name="prefill_third",
    )(q, *tables, done_o, ctx, chip)


def split_units(kv_local):
    order = [(0, 0), (0, 3), (0, 1), (0, 2)]
    units = [(k, i) for k in range(kv_local) for _, i in order]
    first, second = len(units) // 4, len(units) // 2
    return units[:first], units[first:second], units[second:]


def decode_kernel(sections, seen, pick, keys, values, *refs):
    got, ctx_ref, rows = refs[:sections], refs[sections], refs[sections + 1]
    kv_local = keys.shape[0]
    width = kv_local * GROUP * HEAD_DIM
    for k in range(sections):
        for r in range(CAP):
            at = (k * CAP + r) * STEPS
            rows[at : at + STEPS, :] = got[k][r].astype(jnp.float32)
    all_rows = jnp.dot(pick[...], rows[...].astype(jnp.bfloat16), preferred_element_type=jnp.float32)
    all_rows = all_rows.astype(jnp.bfloat16)

    many = GROUP * ROWS
    new_row = lax.broadcasted_iota(jnp.int32, (many, ROWS), 0) % ROWS
    new_col = lax.broadcasted_iota(jnp.int32, (many, ROWS), 1)
    new_allowed = (new_row // STEPS == new_col // STEPS) & (new_col <= new_row)
    contract = (((1,), (1,)), ((), ()))
    for k in range(kv_local):
        q = jnp.concatenate(
            [all_rows[:, (k * GROUP + g) * HEAD_DIM : (k * GROUP + g + 1) * HEAD_DIM] for g in range(GROUP)], axis=0
        )
        new_keys = all_rows[:, width + k * HEAD_DIM : width + (k + 1) * HEAD_DIM]
        at = width + (kv_local + k) * HEAD_DIM
        new_values = all_rows[:, at : at + HEAD_DIM]
        s = jnp.dot(q, keys[k], preferred_element_type=jnp.float32)
        s = (s.reshape(GROUP, ROWS, TOK_DEV) + seen[...][None]).reshape(many, TOK_DEV)
        s_new = lax.dot_general(q, new_keys, contract, preferred_element_type=jnp.float32)
        s_new = jnp.where(new_allowed, s_new, MASKED)
        m = jnp.maximum(jnp.max(s, axis=1, keepdims=True), jnp.max(s_new, axis=1, keepdims=True))
        p = jnp.exp2((s - m) * EXP2_SCALE)
        p_new = jnp.exp2((s_new - m) * EXP2_SCALE)
        o = jnp.dot(p.astype(jnp.bfloat16), values[k], preferred_element_type=jnp.float32)
        total = o[:, HEAD_DIM:] + jnp.sum(p_new, axis=1, keepdims=True)
        o = o[:, :HEAD_DIM] + jnp.dot(p_new.astype(jnp.bfloat16), new_values, preferred_element_type=jnp.float32)
        o = (o / total).astype(jnp.bfloat16)
        for g in range(GROUP):
            ctx_ref[:, (k * GROUP + g) * HEAD_DIM : (k * GROUP + g + 1) * HEAD_DIM] = o[g * ROWS : (g + 1) * ROWS]


def decode(seen, pick, keys, values, got, sections):
    block = got[0].shape
    width = keys.shape[0] * GROUP * HEAD_DIM
    return pl.pallas_call(
        functools.partial(decode_kernel, sections),
        out_shape=jax.ShapeDtypeStruct((ROWS, width), jnp.bfloat16),
        in_specs=[VMEM_SPEC] * (4 + sections),
        out_specs=VMEM_SPEC,
        scratch_shapes=[pltpu.VMEM((sections * CAP * STEPS, block[2]), jnp.float32)],
        compiler_params=params(),
        name="decode_attention",
    )(seen, pick, keys, values, *got)


def project_kernel(sections, *refs):
    ctxs, wo, out_ref = refs[:sections], refs[sections], refs[-1]
    x = jnp.concatenate([c[...] for c in ctxs], axis=0)
    out_ref[...] = jnp.dot(x, wo[...], preferred_element_type=jnp.float32).astype(out_ref.dtype)


def project(ctxs, wo_half, after, sections, dtype):
    rows = sections * ROWS
    depth, wide = wo_half.shape
    return pl.pallas_call(
        functools.partial(project_kernel, sections),
        out_shape=jax.ShapeDtypeStruct((rows, wide), dtype),
        in_specs=[VMEM_SPEC] * (sections + 1) + [ANY_SPEC] * len(after),
        out_specs=VMEM_SPEC,
        compiler_params=params(),
        cost_estimate=pl.CostEstimate(
            flops=rows * depth * wide * 2, bytes_accessed=depth * wide * 2, transcendentals=0
        ),
        name="project_half",
    )(*ctxs, wo_half, *after)


def spread_rows(flip, spread, rows, held, out_hbm, sem):
    y = jnp.dot(spread[...], rows[...], preferred_element_type=jnp.float32)
    for slot in range(held.shape[0]):
        held[slot] = y[slot * STEPS : (slot + 1) * STEPS].astype(held.dtype)
    copy = pltpu.make_async_copy(held, half_columns(out_hbm, flip), sem)
    copy.start()
    copy.wait()


def spread_own_kernel(done, spread, rows, done_o, ctx_in, out_hbm, ctx_hbm, held, sem, sems):
    del ctx_in
    copies = flushes(done, done_o, ctx_hbm, sems)
    for copy in copies:
        copy.start()
    spread_rows(False, spread, rows, held, out_hbm, sem)
    for copy in copies:
        copy.wait()


def spread_own(done, spread, rows, done_o, ctx, sections):
    shape = (sections * DSLOT, STEPS, rows.shape[1])
    return pl.pallas_call(
        functools.partial(spread_own_kernel, done),
        out_shape=[
            jax.ShapeDtypeStruct(shape[:2] + (2 * shape[2],), jnp.bfloat16),
            jax.ShapeDtypeStruct(ctx.shape, ctx.dtype),
        ],
        in_specs=[VMEM_SPEC] * 3 + [ANY_SPEC],
        out_specs=[ANY_SPEC] * 2,
        scratch_shapes=[
            pltpu.VMEM(shape, jnp.bfloat16),
            pltpu.SemaphoreType.DMA,
            pltpu.SemaphoreType.DMA((len(done),)),
        ],
        input_output_aliases={3: 1},
        compiler_params=params(),
        name="spread_own",
    )(spread, rows, done_o, ctx)


def spread_other_kernel(spread, rows, out_in, out_hbm, held, sem):
    del out_in
    spread_rows(True, spread, rows, held, out_hbm, sem)


def spread_other(spread, rows, out):
    shape = out.shape[:2] + (rows.shape[1],)
    return pl.pallas_call(
        spread_other_kernel,
        out_shape=jax.ShapeDtypeStruct(out.shape, out.dtype),
        in_specs=[VMEM_SPEC] * 2 + [ANY_SPEC],
        out_specs=ANY_SPEC,
        scratch_shapes=[pltpu.VMEM(shape, jnp.bfloat16), pltpu.SemaphoreType.DMA],
        input_output_aliases={2: 0},
        compiler_params=params(),
        name="spread_other",
    )(spread, rows, out)


def swap(x, axis, k):
    count = lax.axis_size(axis)
    return lax.ppermute(x, axis, [(i, i ^ k) for i in range(count)])


def per_device(prefill_q, kv_pool, decode_q, decode_kv, wo_weight, page_pair, slot_owner):
    sections = lax.axis_size("section")
    owner = slot_owner.reshape(-1)
    units = split_units(kv_pool.shape[2] // HEAD_DIM)
    ctx_shape = jax.ShapeDtypeStruct(prefill_q.shape, prefill_q.dtype)

    packed = pack(owner, decode_q, decode_kv, sections)
    got = [packed[0]] + [swap(packed[k], "section", k) for k in range(1, sections)]
    done_o, q_later, bias, keys, values, seen, pick, spread, wo_away = prefill_first(
        units[0], units[1] + units[2], page_pair, owner.reshape(1, -1), prefill_q, kv_pool, wo_weight, packed[0], sections
    )
    tables = (bias, keys, values)
    ctx = decode(seen, pick, keys, values, got, sections)
    ctxs = [ctx] + [swap(ctx, "section", k) for k in range(1, sections)]
    prefill_ctx, done_o, wo_keep = prefill_second(
        units[1], units[0], q_later, tables, done_o, wo_weight, ctx_shape, ctx
    )

    away = project(ctxs, wo_away, [wo_keep], sections, jnp.bfloat16)
    came = swap(away, "tensor", 1)
    keep = project(ctxs, wo_keep, [], sections, jnp.float32)
    chip = keep + came.astype(jnp.float32)
    k = 2
    while k < lax.axis_size("tensor"):
        far = swap(chip.astype(jnp.bfloat16), "tensor", k)
        if k == 2:
            prefill_ctx, done_o, chip = prefill_third(
                units[2], len(units[1]), units[1], q_later, tables, done_o, prefill_ctx, chip
            )
        chip = chip + far.astype(jnp.float32)
        k *= 2
    mine = chip.astype(jnp.bfloat16)
    other = swap(mine, "tensor", 1)
    decode_out, prefill_ctx = spread_own(units[2], spread, mine, done_o, prefill_ctx, sections)
    decode_out = spread_other(spread, other, decode_out)
    return (prefill_ctx, decode_out)


def solution(mesh):
    placed = (
        P(("groups", "section"), "tensor"),
        P(None, ("groups", "section"), "tensor"),
        P(("groups", "section"), None, "tensor"),
        P(None, ("groups", "section"), None, "tensor"),
        P("tensor", "section"),
        P("groups", None),
        P("groups", None),
    )
    return jax.shard_map(
        per_device,
        mesh=mesh,
        in_specs=placed,
        out_specs=(P(("groups", "section"), "tensor"), P("groups", None, "section")),
        check_vma=False,
    )
```

```python
import functools

import jax
import jax.numpy as jnp
from jax import lax
from jax.experimental import pallas as pl
from jax.experimental.pallas import tpu as pltpu
from jax.sharding import PartitionSpec as P

HEAD_DIM = 128
GROUP = 8
PAGE = 16
PAIRS_DEV = 4
STEPS = 4
DSLOT = 8
TOK_DEV = 512
CAP = 2
BLOCK = 128
ROWS = PAIRS_DEV * STEPS
SCALE = HEAD_DIM ** (-0.5)
EXP2_SCALE = SCALE * 1.4426950408889634
MASKED = -1e30
VMEM_LIMIT = 20 * 1024 * 1024
REACH = 2
LATEST = (REACH + 1) * BLOCK

SMEM_SPEC = pl.BlockSpec(memory_space=pltpu.SMEM)
VMEM_SPEC = pl.BlockSpec(memory_space=pltpu.VMEM)
ANY_SPEC = pl.BlockSpec(memory_space=pl.ANY)


def params():
    return pltpu.CompilerParams(vmem_limit_bytes=VMEM_LIMIT)


def in_hbm(x):
    return pltpu.with_memory_space_constraint(x, pltpu.HBM)


def half_columns(ref, flip):
    wide = ref.shape[-1] // 2
    half = lax.axis_index("tensor") % 2
    half = 1 - half if flip else half
    return ref.at[(slice(None),) * (len(ref.shape) - 1) + (pl.ds(pl.multiple_of(half * wide, wide), wide),)]


def half_shape(x):
    return jax.ShapeDtypeStruct((*x.shape[:-1], x.shape[-1] // 2), x.dtype)


def pack_kernel(sections, owner_hbm, q_hbm, kv_hbm, *refs):
    outs = refs[:sections]
    owner, q, kv, packed, sems = refs[sections:]
    copies = [
        pltpu.make_async_copy(owner_hbm, owner, sems.at[0]),
        pltpu.make_async_copy(q_hbm, q, sems.at[1]),
        pltpu.make_async_copy(kv_hbm, kv, sems.at[2]),
    ]
    for copy in copies:
        copy.start()
    here = lax.axis_index("section")
    width, kv_width = q.shape[2], kv.shape[3]
    packed[...] = jnp.zeros_like(packed)
    for copy in copies:
        copy.wait()

    def place(pair, carry):
        slot, rank = carry
        rank = jnp.where(pair % PAIRS_DEV == 0, 0, rank)
        mine = owner[pair] == here

        @pl.when(mine)
        def _():
            to = (pair // PAIRS_DEV) ^ here
            packed[to, rank, :, :width] = q[slot]
            packed[to, rank, :, width : width + kv_width] = kv[0, slot]
            packed[to, rank, :, width + kv_width :] = kv[1, slot]

        step = mine.astype(jnp.int32)
        return slot + step, rank + step

    lax.fori_loop(0, owner.shape[0], place, (jnp.int32(0), jnp.int32(0)))
    for k in range(sections):
        outs[k][...] = packed[k]


def pack(owner, decode_q, decode_kv, sections):
    width = decode_q.shape[2] + 2 * decode_kv.shape[3]
    block = (CAP, STEPS, width)
    return pl.pallas_call(
        functools.partial(pack_kernel, sections),
        out_shape=[jax.ShapeDtypeStruct(block, jnp.bfloat16)] * sections,
        in_specs=[ANY_SPEC] * 3,
        out_specs=[VMEM_SPEC] * sections,
        scratch_shapes=[
            pltpu.SMEM(owner.shape, jnp.int32),
            pltpu.VMEM(decode_q.shape, jnp.bfloat16),
            pltpu.VMEM(decode_kv.shape, jnp.bfloat16),
            pltpu.VMEM((sections,) + block, jnp.bfloat16),
            pltpu.SemaphoreType.DMA((3,)),
        ],
        compiler_params=params(),
        name="pack_queries",
    )(in_hbm(owner), in_hbm(decode_q), in_hbm(decode_kv))


def in_order(arrays):
    return [arrays[0], *arrays[:0:-1]]


def pair_starts(page, here):
    rows = lax.broadcasted_iota(jnp.int32, page.shape, 0)
    starts = [jnp.zeros((1, 1), jnp.int32)]
    for j in range(1, PAIRS_DEV):
        lower = jnp.where((rows == here) & (page[...] < j), 1, 0)
        starts.append(jnp.sum(jnp.sum(lower, axis=1, keepdims=True), axis=0, keepdims=True) * PAGE)
    return starts + [jnp.full((1, 1), TOK_DEV, jnp.int32)]


def prefill_masks(starts, bias):
    for i in range(TOK_DEV // BLOCK):
        low = max(0, i - REACH) * BLOCK
        width = (i + 1) * BLOCK - low
        row = lax.broadcasted_iota(jnp.int32, (BLOCK, 1), 0) + i * BLOCK
        first = jnp.zeros((BLOCK, 1), jnp.int32)
        for j in range(1, PAIRS_DEV):
            first = jnp.where(row >= starts[j], starts[j], first)
        row = lax.broadcasted_iota(jnp.int32, (BLOCK, width), 0) + i * BLOCK
        col = lax.broadcasted_iota(jnp.int32, (BLOCK, width), 1) + low
        bias[i, :, :width] = jnp.where((col <= row) & (col >= first), 0.0, MASKED)


def decode_masks(starts, bias):
    row = lax.broadcasted_iota(jnp.int32, (ROWS, 1), 0) // STEPS
    first, last = jnp.zeros((ROWS, 1), jnp.int32), jnp.zeros((ROWS, 1), jnp.int32)
    for j in range(PAIRS_DEV):
        first = jnp.where(row == j, starts[j], first)
        last = jnp.where(row == j, starts[j + 1], last)
    col = lax.broadcasted_iota(jnp.int32, bias.shape, 1)
    bias[...] = jnp.where((col >= first) & (col < last), 0.0, MASKED)


def owner_tables(owner, here, pick, spread):
    pairs = owner.shape[1]
    down = lax.broadcasted_iota(jnp.int32, (pairs, pairs), 0)
    along = lax.broadcasted_iota(jnp.int32, (pairs, pairs), 1)
    owner_along = jnp.broadcast_to(owner[...], (pairs, pairs))
    owner_down = jnp.sum(jnp.where(down == along, owner_along, 0), axis=1, keepdims=True)
    same = owner_along == owner_down
    slot_rank = jnp.sum(jnp.where(same & (down < along), 1, 0), axis=0, keepdims=True)
    slot = owner[...] * DSLOT + slot_rank

    at_home = down // PAIRS_DEV == along // PAIRS_DEV
    home_rank = jnp.sum(jnp.where(same & at_home & (along < down), 1, 0), axis=1, keepdims=True)
    base = ((owner_down ^ here) * CAP + home_rank) * STEPS
    row = lax.broadcasted_iota(jnp.int32, pick.shape, 0)
    col = lax.broadcasted_iota(jnp.int32, pick.shape, 1)
    pair = lax.broadcasted_iota(jnp.int32, (pairs, 1), 0)
    at = row % STEPS
    for j in range(PAIRS_DEV):
        mine = jnp.sum(jnp.where(pair == here * PAIRS_DEV + j, base, 0), axis=0, keepdims=True)
        at = at + jnp.where(row // STEPS == j, mine, 0)
    pick[...] = (col == at).astype(jnp.float32).astype(pick.dtype)

    wide = spread.shape[1]
    pair = lax.broadcasted_iota(jnp.int32, (pairs, wide), 0)
    place = lax.broadcasted_iota(jnp.int32, (pairs, wide), 1) // STEPS
    holds = place == ((pair // PAIRS_DEV) ^ here) * PAIRS_DEV + pair % PAIRS_DEV
    slot_down = jnp.sum(jnp.where(down == along, jnp.broadcast_to(slot, (pairs, pairs)), 0), axis=1, keepdims=True)
    slot_of_place = jnp.sum(jnp.where(holds, slot_down, 0), axis=0, keepdims=True)
    row = lax.broadcasted_iota(jnp.int32, spread.shape, 0)
    col = lax.broadcasted_iota(jnp.int32, spread.shape, 1)
    spread[...] = (row == slot_of_place * STEPS + col % STEPS).astype(jnp.float32).astype(spread.dtype)


def region(ref, unit):
    k, i = unit
    wide = GROUP * HEAD_DIM
    return ref.at[pl.ds(i * BLOCK, BLOCK), pl.ds(k * wide, wide)]


def attend(unit, q, bias, keys, values, o):
    k, i = unit
    low, high = max(0, i - REACH) * BLOCK, (i + 1) * BLOCK
    width = high - low
    rows = jnp.concatenate([q[:, g * HEAD_DIM : (g + 1) * HEAD_DIM] for g in range(GROUP)], axis=0)
    s = jnp.dot(rows, keys[k, :, low:high], preferred_element_type=jnp.float32)
    s = (s.reshape(GROUP, BLOCK, width) + bias[i, :, :width][None]).reshape(GROUP * BLOCK, width)
    m = jnp.max(s, axis=1, keepdims=True)
    p = jnp.exp2((s - m) * EXP2_SCALE).astype(jnp.bfloat16)
    y = jnp.dot(p, values[k, low:high, :], preferred_element_type=jnp.float32)
    y = (y[:, :HEAD_DIM] / y[:, HEAD_DIM:]).astype(jnp.bfloat16)
    for g in range(GROUP):
        o[:, g * HEAD_DIM : (g + 1) * HEAD_DIM] = y[g * BLOCK : (g + 1) * BLOCK]


def flushes(units, blocks, ctx_hbm, sems):
    return [pltpu.make_async_copy(blocks.at[n], region(ctx_hbm, u), sems.at[n]) for n, u in enumerate(units)]


def first_kernel(
    units, later, page_hbm, owner_hbm, q_hbm, kv_hbm, wo_hbm, after,
    o, q_later, bias, keys, values, seen, pick, spread, wo_half,
    page, owner, kv, q, q_sems, late_sems, sems,
):
    del after
    small = [
        pltpu.make_async_copy(page_hbm, page, sems.at[0]),
        pltpu.make_async_copy(owner_hbm, owner, sems.at[1]),
    ]
    cache = pltpu.make_async_copy(kv_hbm, kv, sems.at[2])
    soon = [pltpu.make_async_copy(region(q_hbm, u), q.at[n], q_sems.at[n]) for n, u in enumerate(units)]
    late = [pltpu.make_async_copy(region(q_hbm, u), q_later.at[n], late_sems.at[n]) for n, u in enumerate(later)]
    weights = pltpu.make_async_copy(half_columns(wo_hbm, True), wo_half, sems.at[3])
    for copy in small + [cache] + soon + [weights] + late:
        copy.start()
    here = lax.axis_index("section")
    for copy in small:
        copy.wait()
    starts = pair_starts(page, here)
    prefill_masks(starts, bias)
    decode_masks(starts, seen)
    owner_tables(owner, here, pick, spread)
    cache.wait()
    for k in range(keys.shape[0]):
        cols = slice(k * HEAD_DIM, (k + 1) * HEAD_DIM)
        keys[k] = kv[0, :, cols].astype(jnp.float32).T.astype(jnp.bfloat16)
        values[k, :, :HEAD_DIM] = kv[1, :, cols]
        values[k, :, HEAD_DIM:] = jnp.ones((TOK_DEV, HEAD_DIM), jnp.bfloat16)
    for n, unit in enumerate(units):
        soon[n].wait()
        attend(unit, q.at[n], bias, keys, values, o.at[n])
    for copy in late + [weights]:
        copy.wait()


def second_kernel(
    units, later, done, q, bias, keys, values, done_o, q_hbm, wo_hbm, after,
    ctx_hbm, o, q_later, wo_half, sems, late_sems, wo_sem,
):
    del after
    copies = flushes(done, done_o, ctx_hbm, sems)
    copies.append(pltpu.make_async_copy(half_columns(wo_hbm, False), wo_half, wo_sem))
    copies += [pltpu.make_async_copy(region(q_hbm, u), q_later.at[n], late_sems.at[n]) for n, u in enumerate(later)]
    for copy in copies:
        copy.start()

    @beside
    def _():
        for n, unit in enumerate(units):
            attend(unit, q.at[n], bias, keys, values, o.at[n])

    for copy in copies:
        copy.wait()


def third_kernel(units, done, q, bias, keys, values, done_o, ctx_in, chip_in, ctx_hbm, o, chip, sems):
    del ctx_in, chip_in, chip
    copies = flushes(done, done_o, ctx_hbm, sems)
    for copy in copies:
        copy.start()

    @beside
    def _():
        for n, unit in enumerate(units):
            attend(unit, q.at[n], bias, keys, values, o.at[n])

    for copy in copies:
        copy.wait()


def unit_cost(units):
    pairs = sum(min(i + 1, REACH + 1) for _, i in units) * GROUP * BLOCK * BLOCK
    return pl.CostEstimate(
        flops=pairs * HEAD_DIM * 8, bytes_accessed=len(units) * BLOCK * GROUP * HEAD_DIM * 4, transcendentals=pairs
    )


def beside(body):
    pl.when(lax.axis_index("section") >= 0)(body)


def block_shape(units):
    return jax.ShapeDtypeStruct((len(units), BLOCK, GROUP * HEAD_DIM), jnp.bfloat16)


def prefill_first(units, later, page_pair, owner, prefill_q, kv_pool, wo, after, sections):
    kv_local = kv_pool.shape[2] // HEAD_DIM
    return pl.pallas_call(
        functools.partial(first_kernel, units, later),
        out_shape=[
            block_shape(units),
            block_shape(later),
            jax.ShapeDtypeStruct((TOK_DEV // BLOCK, BLOCK, LATEST), jnp.float32),
            jax.ShapeDtypeStruct((kv_local, HEAD_DIM, TOK_DEV), jnp.bfloat16),
            jax.ShapeDtypeStruct((kv_local, TOK_DEV, 2 * HEAD_DIM), jnp.bfloat16),
            jax.ShapeDtypeStruct((ROWS, TOK_DEV), jnp.float32),
            jax.ShapeDtypeStruct((ROWS, sections * CAP * STEPS), jnp.bfloat16),
            jax.ShapeDtypeStruct((sections * DSLOT * STEPS, sections * ROWS), jnp.bfloat16),
            half_shape(wo),
        ],
        in_specs=[ANY_SPEC] * 6,
        out_specs=[VMEM_SPEC] * 9,
        scratch_shapes=[
            pltpu.VMEM(page_pair.shape, jnp.int32),
            pltpu.VMEM(owner.shape, jnp.int32),
            pltpu.VMEM(kv_pool.shape, jnp.bfloat16),
            pltpu.VMEM(block_shape(units).shape, jnp.bfloat16),
            pltpu.SemaphoreType.DMA((len(units),)),
            pltpu.SemaphoreType.DMA((len(later),)),
            pltpu.SemaphoreType.DMA((4,)),
        ],
        compiler_params=params(),
        cost_estimate=unit_cost(units),
        name="prefill_first",
    )(in_hbm(page_pair), in_hbm(owner), in_hbm(prefill_q), in_hbm(kv_pool), in_hbm(wo), after)


def prefill_second(units, later, done, q, tables, done_o, prefill_q, wo, after):
    return pl.pallas_call(
        functools.partial(second_kernel, units, later, done),
        out_shape=[
            jax.ShapeDtypeStruct(prefill_q.shape, prefill_q.dtype),
            block_shape(units),
            block_shape(later),
            half_shape(wo),
        ],
        in_specs=[VMEM_SPEC] * 5 + [ANY_SPEC] * 3,
        out_specs=[ANY_SPEC] + [VMEM_SPEC] * 3,
        scratch_shapes=[
            pltpu.SemaphoreType.DMA((len(done),)),
            pltpu.SemaphoreType.DMA((len(later),)),
            pltpu.SemaphoreType.DMA,
        ],
        compiler_params=params(),
        cost_estimate=unit_cost(units),
        name="prefill_second",
    )(q, *tables, done_o, in_hbm(prefill_q), in_hbm(wo), after)


def prefill_third(units, done, q, tables, done_o, ctx, chip):
    return pl.pallas_call(
        functools.partial(third_kernel, units, done),
        out_shape=[
            jax.ShapeDtypeStruct(ctx.shape, ctx.dtype),
            block_shape(units),
            jax.ShapeDtypeStruct(chip.shape, chip.dtype),
        ],
        in_specs=[VMEM_SPEC] * 5 + [ANY_SPEC, VMEM_SPEC],
        out_specs=[ANY_SPEC, VMEM_SPEC, VMEM_SPEC],
        scratch_shapes=[pltpu.SemaphoreType.DMA((len(done),))],
        input_output_aliases={5: 0, 6: 2},
        compiler_params=params(),
        cost_estimate=unit_cost(units),
        name="prefill_third",
    )(q, *tables, done_o, ctx, chip)


def split_units(kv_local):
    order = [(0, 0), (0, 1), (0, 2), (0, 3)]
    units = [(k, i) for k in range(kv_local) for _, i in order]
    first, second = len(units) // 4, len(units) // 2
    return units[:first], units[first:second], units[second:]


def decode_kernel(sections, seen, pick, keys, values, *refs):
    got, (ctx_ref, rows) = in_order(refs[:sections]), refs[sections:]
    kv_local = keys.shape[0]
    width = kv_local * GROUP * HEAD_DIM
    for k in range(sections):
        for r in range(CAP):
            at = (k * CAP + r) * STEPS
            rows[at : at + STEPS, :] = got[k][r].astype(jnp.float32)
    all_rows = jnp.dot(pick[...], rows[...].astype(jnp.bfloat16), preferred_element_type=jnp.float32)
    all_rows = all_rows.astype(jnp.bfloat16)

    many = GROUP * ROWS
    new_row = lax.broadcasted_iota(jnp.int32, (many, ROWS), 0) % ROWS
    new_col = lax.broadcasted_iota(jnp.int32, (many, ROWS), 1)
    new_allowed = (new_row // STEPS == new_col // STEPS) & (new_col <= new_row)
    contract = (((1,), (1,)), ((), ()))
    for k in range(kv_local):
        q = jnp.concatenate(
            [all_rows[:, (k * GROUP + g) * HEAD_DIM : (k * GROUP + g + 1) * HEAD_DIM] for g in range(GROUP)], axis=0
        )
        new_keys = all_rows[:, width + k * HEAD_DIM : width + (k + 1) * HEAD_DIM]
        at = width + (kv_local + k) * HEAD_DIM
        new_values = all_rows[:, at : at + HEAD_DIM]
        s = jnp.dot(q, keys[k], preferred_element_type=jnp.float32)
        s = (s.reshape(GROUP, ROWS, TOK_DEV) + seen[...][None]).reshape(many, TOK_DEV)
        s_new = lax.dot_general(q, new_keys, contract, preferred_element_type=jnp.float32)
        s_new = jnp.where(new_allowed, s_new, MASKED)
        m = jnp.maximum(jnp.max(s, axis=1, keepdims=True), jnp.max(s_new, axis=1, keepdims=True))
        p = jnp.exp2((s - m) * EXP2_SCALE)
        p_new = jnp.exp2((s_new - m) * EXP2_SCALE)
        o = jnp.dot(p.astype(jnp.bfloat16), values[k], preferred_element_type=jnp.float32)
        total = o[:, HEAD_DIM:] + jnp.sum(p_new, axis=1, keepdims=True)
        o = o[:, :HEAD_DIM] + jnp.dot(p_new.astype(jnp.bfloat16), new_values, preferred_element_type=jnp.float32)
        o = (o / total).astype(jnp.bfloat16)
        for g in range(GROUP):
            ctx_ref[:, (k * GROUP + g) * HEAD_DIM : (k * GROUP + g + 1) * HEAD_DIM] = o[g * ROWS : (g + 1) * ROWS]


def decode(seen, pick, keys, values, got, sections):
    block = got[0].shape
    width = keys.shape[0] * GROUP * HEAD_DIM
    return pl.pallas_call(
        functools.partial(decode_kernel, sections),
        out_shape=jax.ShapeDtypeStruct((ROWS, width), jnp.bfloat16),
        in_specs=[VMEM_SPEC] * (4 + sections),
        out_specs=VMEM_SPEC,
        scratch_shapes=[pltpu.VMEM((sections * CAP * STEPS, block[2]), jnp.float32)],
        compiler_params=params(),
        name="decode_attention",
    )(seen, pick, keys, values, *in_order(got))


def project_kernel(sections, *refs):
    ctxs, wo, out_ref = in_order(refs[:sections]), refs[sections], refs[-1]
    x = jnp.concatenate([c[...] for c in ctxs], axis=0)
    out_ref[...] = jnp.dot(x, wo[...], preferred_element_type=jnp.float32).astype(out_ref.dtype)


def project(ctxs, wo_half, after, sections, dtype):
    rows = sections * ROWS
    depth, wide = wo_half.shape
    return pl.pallas_call(
        functools.partial(project_kernel, sections),
        out_shape=jax.ShapeDtypeStruct((rows, wide), dtype),
        in_specs=[VMEM_SPEC] * (sections + 1) + [ANY_SPEC] * len(after),
        out_specs=VMEM_SPEC,
        compiler_params=params(),
        cost_estimate=pl.CostEstimate(flops=rows * depth * wide * 2, bytes_accessed=depth * wide * 2, transcendentals=0),
        name="project_half",
    )(*in_order(ctxs), wo_half, *after)


def spread_rows(flip, spread, rows, held, out_hbm, sem):
    y = jnp.dot(spread[...], rows[...], preferred_element_type=jnp.float32)
    for slot in range(held.shape[0]):
        held[slot] = y[slot * STEPS : (slot + 1) * STEPS].astype(held.dtype)
    copy = pltpu.make_async_copy(held, half_columns(out_hbm, flip), sem)
    copy.start()
    copy.wait()


def spread_own_kernel(done, spread, rows, done_o, ctx_in, out_hbm, ctx_hbm, held, sem, sems):
    del ctx_in
    copies = flushes(done, done_o, ctx_hbm, sems)
    for copy in copies:
        copy.start()
    spread_rows(False, spread, rows, held, out_hbm, sem)
    for copy in copies:
        copy.wait()


def spread_own(done, spread, rows, done_o, ctx, sections):
    shape = (sections * DSLOT, STEPS, rows.shape[1])
    return pl.pallas_call(
        functools.partial(spread_own_kernel, done),
        out_shape=[
            jax.ShapeDtypeStruct(shape[:2] + (2 * shape[2],), jnp.bfloat16),
            jax.ShapeDtypeStruct(ctx.shape, ctx.dtype),
        ],
        in_specs=[VMEM_SPEC] * 3 + [ANY_SPEC],
        out_specs=[ANY_SPEC] * 2,
        scratch_shapes=[
            pltpu.VMEM(shape, jnp.bfloat16),
            pltpu.SemaphoreType.DMA,
            pltpu.SemaphoreType.DMA((len(done),)),
        ],
        input_output_aliases={3: 1},
        compiler_params=params(),
        name="spread_own",
    )(spread, rows, done_o, ctx)


def spread_other_kernel(spread, rows, out_in, out_hbm, held, sem):
    del out_in
    spread_rows(True, spread, rows, held, out_hbm, sem)


def spread_other(spread, rows, out):
    shape = out.shape[:2] + (rows.shape[1],)
    return pl.pallas_call(
        spread_other_kernel,
        out_shape=jax.ShapeDtypeStruct(out.shape, out.dtype),
        in_specs=[VMEM_SPEC] * 2 + [ANY_SPEC],
        out_specs=ANY_SPEC,
        scratch_shapes=[pltpu.VMEM(shape, jnp.bfloat16), pltpu.SemaphoreType.DMA],
        input_output_aliases={2: 0},
        compiler_params=params(),
        name="spread_other",
    )(spread, rows, out)


def swap(x, axis, k):
    count = lax.axis_size(axis)
    return lax.ppermute(x, axis, [(i, i ^ k) for i in range(count)])


def per_device(prefill_q, kv_pool, decode_q, decode_kv, wo_weight, page_pair, slot_owner):
    sections = lax.axis_size("section")
    owner = slot_owner.reshape(-1)
    units = split_units(kv_pool.shape[2] // HEAD_DIM)

    packed = pack(owner, decode_q, decode_kv, sections)
    got = [packed[0]] + [swap(packed[k], "section", k) for k in range(1, sections)]
    done_o, q_later, bias, keys, values, seen, pick, spread, wo_away = prefill_first(
        units[0], units[1], page_pair, owner.reshape(1, -1), prefill_q, kv_pool, wo_weight, packed[0], sections
    )
    tables = (bias, keys, values)
    ctx = decode(seen, pick, keys, values, got, sections)
    ctxs = [ctx] + [swap(ctx, "section", k) for k in range(1, sections)]
    prefill_ctx, done_o, q_later, wo_keep = prefill_second(
        units[1], units[2], units[0], q_later, tables, done_o, prefill_q, wo_weight, ctx
    )

    away = project(ctxs, wo_away, [wo_keep], sections, jnp.bfloat16)
    came = swap(away, "tensor", 1)
    keep = project(ctxs, wo_keep, [], sections, jnp.float32)
    chip = keep + came.astype(jnp.float32)
    k = 2
    while k < lax.axis_size("tensor"):
        far = swap(chip.astype(jnp.bfloat16), "tensor", k)
        if k == 2:
            prefill_ctx, done_o, chip = prefill_third(
                units[2], units[1], q_later, tables, done_o, prefill_ctx, chip
            )
        chip = chip + far.astype(jnp.float32)
        k *= 2
    mine = chip.astype(jnp.bfloat16)
    other = swap(mine, "tensor", 1)
    decode_out, prefill_ctx = spread_own(units[2], spread, mine, done_o, prefill_ctx, sections)
    decode_out = spread_other(spread, other, decode_out)
    return (prefill_ctx, decode_out)


def solution(mesh):
    placed = (
        P(("groups", "section"), "tensor"),
        P(None, ("groups", "section"), "tensor"),
        P(("groups", "section"), None, "tensor"),
        P(None, ("groups", "section"), None, "tensor"),
        P("tensor", "section"),
        P("groups", None),
        P("groups", None),
    )
    return jax.shard_map(
        per_device,
        mesh=mesh,
        in_specs=placed,
        out_specs=(P(("groups", "section"), "tensor"), P("groups", None, "section")),
        check_vma=False,
    )
```

```python
import functools

import jax
import jax.numpy as jnp
from jax import lax
from jax.experimental import pallas as pl
from jax.experimental.pallas import tpu as pltpu
from jax.sharding import PartitionSpec as P

HEAD_DIM = 128
GROUP = 8
PAGE = 16
PAIRS_DEV = 4
STEPS = 4
DSLOT = 8
TOK_DEV = 512
CAP = 2
BLOCK = 128
ROWS = PAIRS_DEV * STEPS
SCALE = HEAD_DIM ** (-0.5)
EXP2_SCALE = SCALE * 1.4426950408889634
MASKED = -1e30
VMEM_LIMIT = 20 * 1024 * 1024
REACH = 2
LATEST = (REACH + 1) * BLOCK

SMEM_SPEC = pl.BlockSpec(memory_space=pltpu.SMEM)
VMEM_SPEC = pl.BlockSpec(memory_space=pltpu.VMEM)
ANY_SPEC = pl.BlockSpec(memory_space=pl.ANY)


def params():
    return pltpu.CompilerParams(vmem_limit_bytes=VMEM_LIMIT)


def in_hbm(x):
    return pltpu.with_memory_space_constraint(x, pltpu.HBM)


FIRST_ROUND = ((0, 1, 2, 3), (1, 3, 0, 2), (3, 2, 1, 0), (2, 0, 3, 1))
SECOND_ROUND = ((0, 1, 2, 3), (3, 2, 1, 0), (2, 3, 0, 1), (1, 0, 3, 2))


def routes(table, sections):
    if sections == len(table):
        return table
    return tuple(tuple(i ^ k for i in range(sections)) for k in range(sections))


def back(route):
    return tuple(route.index(i) for i in range(len(route)))


def entry(route, here):
    if all(to == i ^ route[0] for i, to in enumerate(route)):
        return here ^ route[0]
    value = jnp.int32(route[0])
    for i, to in enumerate(route[1:], 1):
        value = jnp.where(here == i, to, value)
    return value


def arrival(round_routes, here, source):
    at = jnp.zeros_like(source)
    for k, route in enumerate(round_routes):
        at = at + jnp.where(source == entry(back(route), here), k, 0)
    return at


def send(x, route):
    return lax.ppermute(x, "section", list(enumerate(route)))


def half_columns(ref, flip):
    wide = ref.shape[-1] // 2
    half = lax.axis_index("tensor") % 2
    half = 1 - half if flip else half
    return ref.at[(slice(None),) * (len(ref.shape) - 1) + (pl.ds(pl.multiple_of(half * wide, wide), wide),)]


def half_shape(x):
    return jax.ShapeDtypeStruct((*x.shape[:-1], x.shape[-1] // 2), x.dtype)


def beside(body):
    pl.when(lax.axis_index("section") >= 0)(body)


def pack_kernel(sections, owner_hbm, q_hbm, kv_hbm, *refs):
    outs = refs[:sections]
    owner, before, q, kv, sems = refs[sections:]
    copies = [
        pltpu.make_async_copy(owner_hbm, owner, sems.at[0]),
        pltpu.make_async_copy(q_hbm, q, sems.at[1]),
        pltpu.make_async_copy(kv_hbm, kv, sems.at[2]),
    ]
    for copy in copies:
        copy.start()
    here = lax.axis_index("section")
    width, kv_width = q.shape[2], kv.shape[3]
    for k in range(sections):
        outs[k][...] = jnp.zeros_like(outs[k])
    copies[0].wait()

    def place(pair, slot):
        before[pair] = slot
        return slot + (owner[pair] == here).astype(jnp.int32)

    lax.fori_loop(0, owner.shape[0], place, jnp.int32(0), unroll=min(owner.shape[0], 16))
    for copy in copies[1:]:
        copy.wait()
    for k in range(sections):
        home = entry(routes(FIRST_ROUND, sections)[k], here) * PAIRS_DEV
        for j in range(PAIRS_DEV):

            @pl.when(owner[home + j] == here)
            def _():
                slot = before[home + j]
                rank = slot - before[home]
                outs[k][rank, :, :width] = q[slot]
                outs[k][rank, :, width : width + kv_width] = kv[0, slot]
                outs[k][rank, :, width + kv_width :] = kv[1, slot]


def pack(owner, decode_q, decode_kv, sections):
    width = decode_q.shape[2] + 2 * decode_kv.shape[3]
    block = (CAP, STEPS, width)
    return pl.pallas_call(
        functools.partial(pack_kernel, sections),
        out_shape=[jax.ShapeDtypeStruct(block, jnp.bfloat16)] * sections,
        in_specs=[ANY_SPEC] * 3,
        out_specs=[VMEM_SPEC] * sections,
        scratch_shapes=[
            pltpu.SMEM(owner.shape, jnp.int32),
            pltpu.SMEM(owner.shape, jnp.int32),
            pltpu.VMEM(decode_q.shape, jnp.bfloat16),
            pltpu.VMEM(decode_kv.shape, jnp.bfloat16),
            pltpu.SemaphoreType.DMA((3,)),
        ],
        compiler_params=params(),
        name="pack_queries",
    )(in_hbm(owner), in_hbm(decode_q), in_hbm(decode_kv))


def pair_starts(page, here):
    rows = lax.broadcasted_iota(jnp.int32, page.shape, 0)
    starts = [jnp.zeros((1, 1), jnp.int32)]
    for j in range(1, PAIRS_DEV):
        lower = jnp.where((rows == here) & (page[...] < j), 1, 0)
        starts.append(jnp.sum(jnp.sum(lower, axis=1, keepdims=True), axis=0, keepdims=True) * PAGE)
    return starts + [jnp.full((1, 1), TOK_DEV, jnp.int32)]


def prefill_masks(starts, bias):
    for i in range(TOK_DEV // BLOCK):
        low = max(0, i - REACH) * BLOCK
        width = (i + 1) * BLOCK - low
        row = lax.broadcasted_iota(jnp.int32, (BLOCK, 1), 0) + i * BLOCK
        first = jnp.zeros((BLOCK, 1), jnp.int32)
        for j in range(1, PAIRS_DEV):
            first = jnp.where(row >= starts[j], starts[j], first)
        row = lax.broadcasted_iota(jnp.int32, (BLOCK, width), 0) + i * BLOCK
        col = lax.broadcasted_iota(jnp.int32, (BLOCK, width), 1) + low
        bias[i, :, :width] = jnp.where((col <= row) & (col >= first), 0.0, MASKED)


def decode_masks(starts, bias):
    row = lax.broadcasted_iota(jnp.int32, (ROWS, 1), 0) // STEPS
    first, last = jnp.zeros((ROWS, 1), jnp.int32), jnp.zeros((ROWS, 1), jnp.int32)
    for j in range(PAIRS_DEV):
        first = jnp.where(row == j, starts[j], first)
        last = jnp.where(row == j, starts[j + 1], last)
    col = lax.broadcasted_iota(jnp.int32, bias.shape, 1)
    bias[...] = jnp.where((col >= first) & (col < last), 0.0, MASKED)


def owner_grid(owner):
    pairs = owner.shape[1]
    down = lax.broadcasted_iota(jnp.int32, (pairs, pairs), 0)
    along = lax.broadcasted_iota(jnp.int32, (pairs, pairs), 1)
    owner_along = jnp.broadcast_to(owner[...], (pairs, pairs))
    owner_down = jnp.sum(jnp.where(down == along, owner_along, 0), axis=1, keepdims=True)
    return down, along, owner_down, owner_along == owner_down


def home_rows(sections, owner, here, pick):
    down, along, owner_down, same = owner_grid(owner)
    at_home = down // PAIRS_DEV == along // PAIRS_DEV
    home_rank = jnp.sum(jnp.where(same & at_home & (along < down), 1, 0), axis=1, keepdims=True)
    base = (arrival(routes(FIRST_ROUND, sections), here, owner_down) * CAP + home_rank) * STEPS
    row = lax.broadcasted_iota(jnp.int32, pick.shape, 0)
    col = lax.broadcasted_iota(jnp.int32, pick.shape, 1)
    pair = lax.broadcasted_iota(jnp.int32, base.shape, 0)
    at = row % STEPS
    for j in range(PAIRS_DEV):
        mine = jnp.sum(jnp.where(pair == here * PAIRS_DEV + j, base, 0), axis=0, keepdims=True)
        at = at + jnp.where(row // STEPS == j, mine, 0)
    pick[...] = (col == at).astype(jnp.float32).astype(pick.dtype)


def slot_rows(sections, owner, here, spread):
    down, along, _, same = owner_grid(owner)
    slot_rank = jnp.sum(jnp.where(same & (down < along), 1, 0), axis=0, keepdims=True)
    slot_along = jnp.broadcast_to(owner[...] * DSLOT + slot_rank, down.shape)
    slot_down = jnp.sum(jnp.where(down == along, slot_along, 0), axis=1, keepdims=True)
    shape = (down.shape[0], spread.shape[1])
    pair = lax.broadcasted_iota(jnp.int32, shape, 0)
    place = lax.broadcasted_iota(jnp.int32, shape, 1) // STEPS
    position = arrival(routes(SECOND_ROUND, sections), here, pair // PAIRS_DEV)
    holds = place == position * PAIRS_DEV + pair % PAIRS_DEV
    slot_of_place = jnp.sum(jnp.where(holds, slot_down, 0), axis=0, keepdims=True)
    row = lax.broadcasted_iota(jnp.int32, spread.shape, 0)
    col = lax.broadcasted_iota(jnp.int32, spread.shape, 1)
    spread[...] = (row == slot_of_place * STEPS + col % STEPS).astype(jnp.float32).astype(spread.dtype)


def region(ref, unit):
    k, i = unit
    wide = GROUP * HEAD_DIM
    return ref.at[pl.ds(i * BLOCK, BLOCK), pl.ds(k * wide, wide)]


def attend(unit, q, bias, keys, values, o):
    k, i = unit
    low, high = max(0, i - REACH) * BLOCK, (i + 1) * BLOCK
    width = high - low
    rows = jnp.concatenate([q[:, g * HEAD_DIM : (g + 1) * HEAD_DIM] for g in range(GROUP)], axis=0)
    s = jnp.dot(rows, keys[k, :, low:high], preferred_element_type=jnp.float32)
    s = (s.reshape(GROUP, BLOCK, width) + bias[i, :, :width][None]).reshape(GROUP * BLOCK, width)
    m = jnp.max(s, axis=1, keepdims=True)
    p = jnp.exp2((s - m) * EXP2_SCALE).astype(jnp.bfloat16)
    y = jnp.dot(p, values[k, low:high, :], preferred_element_type=jnp.float32)
    y = (y[:, :HEAD_DIM] / y[:, HEAD_DIM:]).astype(jnp.bfloat16)
    for g in range(GROUP):
        o[:, g * HEAD_DIM : (g + 1) * HEAD_DIM] = y[g * BLOCK : (g + 1) * BLOCK]


def flushes(units, blocks, ctx_hbm, sems):
    return [pltpu.make_async_copy(blocks.at[n], region(ctx_hbm, u), sems.at[n]) for n, u in enumerate(units)]


def tables_kernel(
    sections, units, page_hbm, owner_hbm, kv_hbm, q_hbm, after,
    page, owner, keys, values, seen, pick, q, kv, sems, q_sems,
):
    del after
    copies = [
        pltpu.make_async_copy(page_hbm, page, sems.at[0]),
        pltpu.make_async_copy(owner_hbm, owner, sems.at[1]),
        pltpu.make_async_copy(kv_hbm, kv, sems.at[2]),
    ]
    later = [pltpu.make_async_copy(region(q_hbm, u), q.at[n], q_sems.at[n]) for n, u in enumerate(units)]
    for copy in copies + later:
        copy.start()
    here = lax.axis_index("section")
    for copy in copies:
        copy.wait()

    @beside
    def _():
        decode_masks(pair_starts(page, here), seen)
        home_rows(sections, owner, here, pick)
        for k in range(keys.shape[0]):
            cols = slice(k * HEAD_DIM, (k + 1) * HEAD_DIM)
            keys[k] = kv[0, :, cols].astype(jnp.float32).T.astype(jnp.bfloat16)
            values[k, :, :HEAD_DIM] = kv[1, :, cols]
            values[k, :, HEAD_DIM:] = jnp.ones((TOK_DEV, HEAD_DIM), jnp.bfloat16)

    for copy in later:
        copy.wait()


def first_kernel(
    sections, units, later, page, owner, q, keys, values, q_hbm, after,
    o, q_later, bias, spread, sems,
):
    del after
    copies = [pltpu.make_async_copy(region(q_hbm, u), q_later.at[n], sems.at[n]) for n, u in enumerate(later)]
    for copy in copies:
        copy.start()

    @beside
    def _():
        here = lax.axis_index("section")
        prefill_masks(pair_starts(page, here), bias)
        slot_rows(sections, owner, here, spread)
        for n, unit in enumerate(units):
            attend(unit, q.at[n], bias, keys, values, o.at[n])

    for copy in copies:
        copy.wait()


def second_kernel(units, done, q, bias, keys, values, done_o, chip_in, ctx_hbm, o, chip, sems):
    del chip_in, chip
    copies = flushes(done, done_o, ctx_hbm, sems)
    for copy in copies:
        copy.start()

    @beside
    def _():
        for n, unit in enumerate(units):
            attend(unit, q.at[n], bias, keys, values, o.at[n])

    for copy in copies:
        copy.wait()


def unit_cost(units):
    pairs = sum(min(i + 1, REACH + 1) for _, i in units) * GROUP * BLOCK * BLOCK
    return pl.CostEstimate(
        flops=pairs * HEAD_DIM * 8, bytes_accessed=len(units) * BLOCK * GROUP * HEAD_DIM * 4, transcendentals=pairs
    )


def block_shape(units):
    return jax.ShapeDtypeStruct((len(units), BLOCK, GROUP * HEAD_DIM), jnp.bfloat16)


def make_tables(units, page_pair, owner, kv_pool, prefill_q, after, sections):
    kv_local = kv_pool.shape[2] // HEAD_DIM
    return pl.pallas_call(
        functools.partial(tables_kernel, sections, units),
        out_shape=[
            jax.ShapeDtypeStruct(page_pair.shape, jnp.int32),
            jax.ShapeDtypeStruct(owner.shape, jnp.int32),
            jax.ShapeDtypeStruct((kv_local, HEAD_DIM, TOK_DEV), jnp.bfloat16),
            jax.ShapeDtypeStruct((kv_local, TOK_DEV, 2 * HEAD_DIM), jnp.bfloat16),
            jax.ShapeDtypeStruct((ROWS, TOK_DEV), jnp.float32),
            jax.ShapeDtypeStruct((ROWS, sections * CAP * STEPS), jnp.bfloat16),
            block_shape(units),
        ],
        in_specs=[ANY_SPEC] * 5,
        out_specs=[VMEM_SPEC] * 7,
        scratch_shapes=[
            pltpu.VMEM(kv_pool.shape, jnp.bfloat16),
            pltpu.SemaphoreType.DMA((3,)),
            pltpu.SemaphoreType.DMA((len(units),)),
        ],
        compiler_params=params(),
        cost_estimate=unit_cost(units),
        name="make_tables",
    )(in_hbm(page_pair), in_hbm(owner), in_hbm(kv_pool), in_hbm(prefill_q), after)


def prefill_first(units, later, page, owner, q, keys, values, prefill_q, after, sections):
    return pl.pallas_call(
        functools.partial(first_kernel, sections, units, later),
        out_shape=[
            block_shape(units),
            block_shape(later),
            jax.ShapeDtypeStruct((TOK_DEV // BLOCK, BLOCK, LATEST), jnp.float32),
            jax.ShapeDtypeStruct((sections * DSLOT * STEPS, sections * ROWS), jnp.bfloat16),
        ],
        in_specs=[VMEM_SPEC] * 5 + [ANY_SPEC] * 2,
        out_specs=[VMEM_SPEC] * 4,
        scratch_shapes=[pltpu.SemaphoreType.DMA((len(later),))],
        compiler_params=params(),
        cost_estimate=unit_cost(units),
        name="prefill_first",
    )(page, owner, q, keys, values, in_hbm(prefill_q), after)


def prefill_second(units, done, q, bias, keys, values, done_o, ctx_shape, chip):
    return pl.pallas_call(
        functools.partial(second_kernel, units, done),
        out_shape=[ctx_shape, block_shape(units), jax.ShapeDtypeStruct(chip.shape, chip.dtype)],
        in_specs=[VMEM_SPEC] * 6,
        out_specs=[ANY_SPEC, VMEM_SPEC, VMEM_SPEC],
        scratch_shapes=[pltpu.SemaphoreType.DMA((len(done),))],
        input_output_aliases={5: 2},
        compiler_params=params(),
        cost_estimate=unit_cost(units),
        name="prefill_second",
    )(q, bias, keys, values, done_o, chip)


def split_units(kv_local):
    units = [(k, i) for k in range(kv_local) for i in range(TOK_DEV // BLOCK)]
    return units[: len(units) // 2], units[len(units) // 2 :]


def decode_kernel(sections, seen, pick, keys, values, *refs):
    got, (ctx_ref, rows) = refs[:sections], refs[sections:]
    kv_local = keys.shape[0]
    width = kv_local * GROUP * HEAD_DIM
    for k in range(sections):
        for r in range(CAP):
            at = (k * CAP + r) * STEPS
            rows[at : at + STEPS, :] = got[k][r].astype(jnp.float32)
    all_rows = jnp.dot(pick[...], rows[...].astype(jnp.bfloat16), preferred_element_type=jnp.float32)
    all_rows = all_rows.astype(jnp.bfloat16)

    many = GROUP * ROWS
    new_row = lax.broadcasted_iota(jnp.int32, (many, ROWS), 0) % ROWS
    new_col = lax.broadcasted_iota(jnp.int32, (many, ROWS), 1)
    new_allowed = (new_row // STEPS == new_col // STEPS) & (new_col <= new_row)
    contract = (((1,), (1,)), ((), ()))
    for k in range(kv_local):
        q = jnp.concatenate(
            [all_rows[:, (k * GROUP + g) * HEAD_DIM : (k * GROUP + g + 1) * HEAD_DIM] for g in range(GROUP)], axis=0
        )
        new_keys = all_rows[:, width + k * HEAD_DIM : width + (k + 1) * HEAD_DIM]
        at = width + (kv_local + k) * HEAD_DIM
        new_values = all_rows[:, at : at + HEAD_DIM]
        s = jnp.dot(q, keys[k], preferred_element_type=jnp.float32)
        s = (s.reshape(GROUP, ROWS, TOK_DEV) + seen[...][None]).reshape(many, TOK_DEV)
        s_new = lax.dot_general(q, new_keys, contract, preferred_element_type=jnp.float32)
        s_new = jnp.where(new_allowed, s_new, MASKED)
        m = jnp.maximum(jnp.max(s, axis=1, keepdims=True), jnp.max(s_new, axis=1, keepdims=True))
        p = jnp.exp2((s - m) * EXP2_SCALE)
        p_new = jnp.exp2((s_new - m) * EXP2_SCALE)
        o = jnp.dot(p.astype(jnp.bfloat16), values[k], preferred_element_type=jnp.float32)
        total = o[:, HEAD_DIM:] + jnp.sum(p_new, axis=1, keepdims=True)
        o = o[:, :HEAD_DIM] + jnp.dot(p_new.astype(jnp.bfloat16), new_values, preferred_element_type=jnp.float32)
        o = (o / total).astype(jnp.bfloat16)
        for g in range(GROUP):
            ctx_ref[:, (k * GROUP + g) * HEAD_DIM : (k * GROUP + g + 1) * HEAD_DIM] = o[g * ROWS : (g + 1) * ROWS]


def decode(seen, pick, keys, values, got, sections):
    block = got[0].shape
    width = keys.shape[0] * GROUP * HEAD_DIM
    return pl.pallas_call(
        functools.partial(decode_kernel, sections),
        out_shape=jax.ShapeDtypeStruct((ROWS, width), jnp.bfloat16),
        in_specs=[VMEM_SPEC] * (4 + sections),
        out_specs=VMEM_SPEC,
        scratch_shapes=[pltpu.VMEM((sections * CAP * STEPS, block[2]), jnp.float32)],
        compiler_params=params(),
        name="decode_attention",
    )(seen, pick, keys, values, *got)


def project_kernel(sections, flip, *refs):
    ctxs, wo, out_ref = refs[:sections][::-1], refs[sections], refs[-1]
    x = jnp.concatenate([c[...] for c in ctxs], axis=0)
    rows = x.shape[0]
    if rows < BLOCK:
        x = jnp.concatenate([x] * (BLOCK // rows), axis=0)
    out_ref[...] = jnp.dot(x, half_columns(wo, flip)[...], preferred_element_type=jnp.float32)[:rows].astype(out_ref.dtype)


def project(flip, ctxs, wo, after, sections, dtype):
    rows = sections * ROWS
    depth, wide = wo.shape[0], wo.shape[1] // 2
    return pl.pallas_call(
        functools.partial(project_kernel, sections, flip),
        out_shape=jax.ShapeDtypeStruct((rows, wide), dtype),
        in_specs=[VMEM_SPEC] * (sections + 1) + [ANY_SPEC] * len(after),
        out_specs=VMEM_SPEC,
        compiler_params=params(),
        cost_estimate=pl.CostEstimate(flops=rows * depth * wide * 2, bytes_accessed=depth * wide * 2, transcendentals=0),
        name="project_half",
    )(*ctxs[::-1], wo, *after)


def spread_rows(flip, spread, rows, held, out_hbm, sem):
    y = jnp.dot(spread[...], rows[...], preferred_element_type=jnp.float32)
    for slot in range(held.shape[0]):
        held[slot] = y[slot * STEPS : (slot + 1) * STEPS].astype(held.dtype)
    copy = pltpu.make_async_copy(held, half_columns(out_hbm, flip), sem)
    copy.start()
    copy.wait()


def spread_own_kernel(done, spread, rows, done_o, ctx_in, out_hbm, ctx_hbm, held, sem, sems):
    del ctx_in
    copies = flushes(done, done_o, ctx_hbm, sems)
    for copy in copies:
        copy.start()
    spread_rows(False, spread, rows, held, out_hbm, sem)
    for copy in copies:
        copy.wait()


def spread_own(done, spread, rows, done_o, ctx, sections):
    shape = (sections * DSLOT, STEPS, rows.shape[1])
    return pl.pallas_call(
        functools.partial(spread_own_kernel, done),
        out_shape=[
            jax.ShapeDtypeStruct(shape[:2] + (2 * shape[2],), jnp.bfloat16),
            jax.ShapeDtypeStruct(ctx.shape, ctx.dtype),
        ],
        in_specs=[VMEM_SPEC] * 3 + [ANY_SPEC],
        out_specs=[ANY_SPEC] * 2,
        scratch_shapes=[
            pltpu.VMEM(shape, jnp.bfloat16),
            pltpu.SemaphoreType.DMA,
            pltpu.SemaphoreType.DMA((len(done),)),
        ],
        input_output_aliases={3: 1},
        compiler_params=params(),
        name="spread_own",
    )(spread, rows, done_o, ctx)


def spread_other_kernel(spread, rows, out_in, out_hbm, held, sem):
    del out_in
    spread_rows(True, spread, rows, held, out_hbm, sem)


def spread_other(spread, rows, out):
    shape = out.shape[:2] + (rows.shape[1],)
    return pl.pallas_call(
        spread_other_kernel,
        out_shape=jax.ShapeDtypeStruct(out.shape, out.dtype),
        in_specs=[VMEM_SPEC] * 2 + [ANY_SPEC],
        out_specs=ANY_SPEC,
        scratch_shapes=[pltpu.VMEM(shape, jnp.bfloat16), pltpu.SemaphoreType.DMA],
        input_output_aliases={2: 0},
        compiler_params=params(),
        name="spread_other",
    )(spread, rows, out)


def swap(x, axis, k):
    count = lax.axis_size(axis)
    return lax.ppermute(x, axis, [(i, i ^ k) for i in range(count)])


def per_device(prefill_q, kv_pool, decode_q, decode_kv, wo_weight, page_pair, slot_owner):
    sections = lax.axis_size("section")
    owner = slot_owner.reshape(-1)
    units = split_units(kv_pool.shape[2] // HEAD_DIM)
    ctx_shape = jax.ShapeDtypeStruct(prefill_q.shape, prefill_q.dtype)

    packed = pack(owner, decode_q, decode_kv, sections)
    first, second = routes(FIRST_ROUND, sections), routes(SECOND_ROUND, sections)
    got = [packed[0]] + [send(x, route) for x, route in zip(packed[1:], first[1:])]
    page, owner, keys, values, seen, pick, q = make_tables(
        units[0], page_pair, owner.reshape(1, -1), kv_pool, prefill_q, packed[0], sections
    )
    ctx = decode(seen, pick, keys, values, got, sections)
    ctxs = [ctx] + [send(ctx, route) for route in second[1:]]
    done_o, q, bias, spread = prefill_first(
        units[0], units[1], page, owner, q, keys, values, prefill_q, ctx, sections
    )

    away = project(True, ctxs, wo_weight, [q], sections, jnp.bfloat16)
    came = swap(away, "tensor", 1)
    keep = project(False, ctxs, wo_weight, [], sections, jnp.float32)
    chip = keep + came.astype(jnp.float32)
    k = 2
    while k < lax.axis_size("tensor"):
        far = swap(chip.astype(jnp.bfloat16), "tensor", k)
        if k == 2:
            prefill_ctx, done_o, chip = prefill_second(
                units[1], units[0], q, bias, keys, values, done_o, ctx_shape, chip
            )
        chip = chip + far.astype(jnp.float32)
        k *= 2
    mine = chip.astype(jnp.bfloat16)
    other = swap(mine, "tensor", 1)
    decode_out, prefill_ctx = spread_own(units[1], spread, mine, done_o, prefill_ctx, sections)
    decode_out = spread_other(spread, other, decode_out)
    return (prefill_ctx, decode_out)


def solution(mesh):
    placed = (
        P(("groups", "section"), "tensor"),
        P(None, ("groups", "section"), "tensor"),
        P(("groups", "section"), None, "tensor"),
        P(None, ("groups", "section"), None, "tensor"),
        P("tensor", "section"),
        P("groups", None),
        P("groups", None),
    )
    return jax.shard_map(
        per_device,
        mesh=mesh,
        in_specs=placed,
        out_specs=(P(("groups", "section"), "tensor"), P("groups", None, "section")),
        check_vma=False,
    )
```

```python
import functools

import jax
import jax.numpy as jnp
from jax import lax
from jax.experimental import pallas as pl
from jax.experimental.pallas import tpu as pltpu
from jax.sharding import PartitionSpec as P

HEAD_DIM = 128
GROUP = 8
PAGE = 16
PAIRS_DEV = 4
STEPS = 4
DSLOT = 8
TOK_DEV = 512
CAP = 2
BLOCK = 128
ROWS = PAIRS_DEV * STEPS
SCALE = HEAD_DIM ** (-0.5)
EXP2_SCALE = SCALE * 1.4426950408889634
MASKED = -1e30
VMEM_LIMIT = 20 * 1024 * 1024
REACH = 2
LATEST = (REACH + 1) * BLOCK

SMEM_SPEC = pl.BlockSpec(memory_space=pltpu.SMEM)
VMEM_SPEC = pl.BlockSpec(memory_space=pltpu.VMEM)
ANY_SPEC = pl.BlockSpec(memory_space=pl.ANY)


def params():
    return pltpu.CompilerParams(vmem_limit_bytes=VMEM_LIMIT)


def in_hbm(x):
    return pltpu.with_memory_space_constraint(x, pltpu.HBM)


FIRST_ROUND = ((0, 1, 2, 3), (1, 2, 3, 0), (2, 3, 0, 1), (3, 0, 1, 2))
SECOND_ROUND = ((0, 1, 2, 3), (1, 3, 0, 2), (3, 2, 1, 0), (2, 0, 3, 1))


def routes(table, sections):
    if sections == len(table):
        return table
    return tuple(tuple(i ^ k for i in range(sections)) for k in range(sections))


def back(route):
    return tuple(route.index(i) for i in range(len(route)))


def entry(route, here):
    if all(to == i ^ route[0] for i, to in enumerate(route)):
        return here ^ route[0]
    value = jnp.int32(route[0])
    for i, to in enumerate(route[1:], 1):
        value = jnp.where(here == i, to, value)
    return value


def arrival(round_routes, here, source):
    at = jnp.zeros_like(source)
    for k, route in enumerate(round_routes):
        at = at + jnp.where(source == entry(back(route), here), k, 0)
    return at


def send(x, route):
    return lax.ppermute(x, "section", list(enumerate(route)))


def half_columns(ref, flip):
    wide = ref.shape[-1] // 2
    half = lax.axis_index("tensor") % 2
    half = 1 - half if flip else half
    return ref.at[(slice(None),) * (len(ref.shape) - 1) + (pl.ds(pl.multiple_of(half * wide, wide), wide),)]


def half_shape(x):
    return jax.ShapeDtypeStruct((*x.shape[:-1], x.shape[-1] // 2), x.dtype)


def beside(body):
    pl.when(lax.axis_index("section") >= 0)(body)


def pack_kernel(sections, owner_hbm, q_hbm, kv_hbm, *refs):
    outs = refs[:sections]
    owner, before, q, kv, sems = refs[sections:]
    copies = [
        pltpu.make_async_copy(owner_hbm, owner, sems.at[0]),
        pltpu.make_async_copy(q_hbm, q, sems.at[1]),
        pltpu.make_async_copy(kv_hbm, kv, sems.at[2]),
    ]
    for copy in copies:
        copy.start()
    here = lax.axis_index("section")
    width, kv_width = q.shape[2], kv.shape[3]
    for k in range(sections):
        outs[k][...] = jnp.zeros_like(outs[k])
    copies[0].wait()

    def place(pair, slot):
        before[pair] = slot
        return slot + (owner[pair] == here).astype(jnp.int32)

    lax.fori_loop(0, owner.shape[0], place, jnp.int32(0), unroll=min(owner.shape[0], 16))
    for copy in copies[1:]:
        copy.wait()
    for k in range(sections):
        home = entry(routes(FIRST_ROUND, sections)[k], here) * PAIRS_DEV
        for j in range(PAIRS_DEV):

            @pl.when(owner[home + j] == here)
            def _():
                slot = before[home + j]
                rank = slot - before[home]
                outs[k][rank, :, :width] = q[slot]
                outs[k][rank, :, width : width + kv_width] = kv[0, slot]
                outs[k][rank, :, width + kv_width :] = kv[1, slot]


def pack(owner, decode_q, decode_kv, sections):
    width = decode_q.shape[2] + 2 * decode_kv.shape[3]
    block = (CAP, STEPS, width)
    return pl.pallas_call(
        functools.partial(pack_kernel, sections),
        out_shape=[jax.ShapeDtypeStruct(block, jnp.bfloat16)] * sections,
        in_specs=[ANY_SPEC] * 3,
        out_specs=[VMEM_SPEC] * sections,
        scratch_shapes=[
            pltpu.SMEM(owner.shape, jnp.int32),
            pltpu.SMEM(owner.shape, jnp.int32),
            pltpu.VMEM(decode_q.shape, jnp.bfloat16),
            pltpu.VMEM(decode_kv.shape, jnp.bfloat16),
            pltpu.SemaphoreType.DMA((3,)),
        ],
        compiler_params=params(),
        name="pack_queries",
    )(in_hbm(owner), in_hbm(decode_q), in_hbm(decode_kv))


def pair_starts(page, here):
    rows = lax.broadcasted_iota(jnp.int32, page.shape, 0)
    starts = [jnp.zeros((1, 1), jnp.int32)]
    for j in range(1, PAIRS_DEV):
        lower = jnp.where((rows == here) & (page[...] < j), 1, 0)
        starts.append(jnp.sum(jnp.sum(lower, axis=1, keepdims=True), axis=0, keepdims=True) * PAGE)
    return starts + [jnp.full((1, 1), TOK_DEV, jnp.int32)]


def prefill_masks(starts, bias):
    for i in range(TOK_DEV // BLOCK):
        low = max(0, i - REACH) * BLOCK
        width = (i + 1) * BLOCK - low
        row = lax.broadcasted_iota(jnp.int32, (BLOCK, 1), 0) + i * BLOCK
        first = jnp.zeros((BLOCK, 1), jnp.int32)
        for j in range(1, PAIRS_DEV):
            first = jnp.where(row >= starts[j], starts[j], first)
        row = lax.broadcasted_iota(jnp.int32, (BLOCK, width), 0) + i * BLOCK
        col = lax.broadcasted_iota(jnp.int32, (BLOCK, width), 1) + low
        bias[i, :, :width] = jnp.where((col <= row) & (col >= first), 0.0, MASKED)


def decode_masks(starts, bias):
    row = lax.broadcasted_iota(jnp.int32, (ROWS, 1), 0) // STEPS
    first, last = jnp.zeros((ROWS, 1), jnp.int32), jnp.zeros((ROWS, 1), jnp.int32)
    for j in range(PAIRS_DEV):
        first = jnp.where(row == j, starts[j], first)
        last = jnp.where(row == j, starts[j + 1], last)
    col = lax.broadcasted_iota(jnp.int32, bias.shape, 1)
    bias[...] = jnp.where((col >= first) & (col < last), 0.0, MASKED)


def owner_grid(owner):
    pairs = owner.shape[1]
    down = lax.broadcasted_iota(jnp.int32, (pairs, pairs), 0)
    along = lax.broadcasted_iota(jnp.int32, (pairs, pairs), 1)
    owner_along = jnp.broadcast_to(owner[...], (pairs, pairs))
    owner_down = jnp.sum(jnp.where(down == along, owner_along, 0), axis=1, keepdims=True)
    return down, along, owner_down, owner_along == owner_down


def home_rows(sections, owner, here, pick):
    down, along, owner_down, same = owner_grid(owner)
    at_home = down // PAIRS_DEV == along // PAIRS_DEV
    home_rank = jnp.sum(jnp.where(same & at_home & (along < down), 1, 0), axis=1, keepdims=True)
    base = (arrival(routes(FIRST_ROUND, sections), here, owner_down) * CAP + home_rank) * STEPS
    row = lax.broadcasted_iota(jnp.int32, pick.shape, 0)
    col = lax.broadcasted_iota(jnp.int32, pick.shape, 1)
    pair = lax.broadcasted_iota(jnp.int32, base.shape, 0)
    at = row % STEPS
    for j in range(PAIRS_DEV):
        mine = jnp.sum(jnp.where(pair == here * PAIRS_DEV + j, base, 0), axis=0, keepdims=True)
        at = at + jnp.where(row // STEPS == j, mine, 0)
    pick[...] = (col == at).astype(jnp.float32).astype(pick.dtype)


def slot_rows(sections, owner, here, spread):
    down, along, _, same = owner_grid(owner)
    slot_rank = jnp.sum(jnp.where(same & (down < along), 1, 0), axis=0, keepdims=True)
    slot_along = jnp.broadcast_to(owner[...] * DSLOT + slot_rank, down.shape)
    slot_down = jnp.sum(jnp.where(down == along, slot_along, 0), axis=1, keepdims=True)
    shape = (down.shape[0], spread.shape[1])
    pair = lax.broadcasted_iota(jnp.int32, shape, 0)
    place = lax.broadcasted_iota(jnp.int32, shape, 1) // STEPS
    position = arrival(routes(SECOND_ROUND, sections), here, pair // PAIRS_DEV)
    holds = place == position * PAIRS_DEV + pair % PAIRS_DEV
    slot_of_place = jnp.sum(jnp.where(holds, slot_down, 0), axis=0, keepdims=True)
    row = lax.broadcasted_iota(jnp.int32, spread.shape, 0)
    col = lax.broadcasted_iota(jnp.int32, spread.shape, 1)
    spread[...] = (row == slot_of_place * STEPS + col % STEPS).astype(jnp.float32).astype(spread.dtype)


def region(ref, unit):
    k, i = unit
    wide = GROUP * HEAD_DIM
    return ref.at[pl.ds(i * BLOCK, BLOCK), pl.ds(k * wide, wide)]


def attend(unit, q, bias, keys, values, o):
    k, i = unit
    low, high = max(0, i - REACH) * BLOCK, (i + 1) * BLOCK
    width = high - low
    rows = jnp.concatenate([q[:, g * HEAD_DIM : (g + 1) * HEAD_DIM] for g in range(GROUP)], axis=0)
    s = jnp.dot(rows, keys[k, :, low:high], preferred_element_type=jnp.float32)
    s = (s.reshape(GROUP, BLOCK, width) + bias[i, :, :width][None]).reshape(GROUP * BLOCK, width)
    m = jnp.max(s, axis=1, keepdims=True)
    p = jnp.exp2((s - m) * EXP2_SCALE).astype(jnp.bfloat16)
    y = jnp.dot(p, values[k, low:high, :], preferred_element_type=jnp.float32)
    y = (y[:, :HEAD_DIM] / y[:, HEAD_DIM:]).astype(jnp.bfloat16)
    for g in range(GROUP):
        o[:, g * HEAD_DIM : (g + 1) * HEAD_DIM] = y[g * BLOCK : (g + 1) * BLOCK]


def flushes(units, blocks, ctx_hbm, sems):
    return [pltpu.make_async_copy(blocks.at[n], region(ctx_hbm, u), sems.at[n]) for n, u in enumerate(units)]


def tables_kernel(
    sections, units, page_hbm, owner_hbm, kv_hbm, q_hbm, after,
    page, owner, keys, values, seen, pick, q, kv, sems, q_sems,
):
    del after
    copies = [
        pltpu.make_async_copy(page_hbm, page, sems.at[0]),
        pltpu.make_async_copy(owner_hbm, owner, sems.at[1]),
        pltpu.make_async_copy(kv_hbm, kv, sems.at[2]),
    ]
    later = [pltpu.make_async_copy(region(q_hbm, u), q.at[n], q_sems.at[n]) for n, u in enumerate(units)]
    for copy in copies + later:
        copy.start()
    here = lax.axis_index("section")
    for copy in copies:
        copy.wait()

    @beside
    def _():
        decode_masks(pair_starts(page, here), seen)
        home_rows(sections, owner, here, pick)
        for k in range(keys.shape[0]):
            cols = slice(k * HEAD_DIM, (k + 1) * HEAD_DIM)
            keys[k] = kv[0, :, cols].astype(jnp.float32).T.astype(jnp.bfloat16)
            values[k, :, :HEAD_DIM] = kv[1, :, cols]
            values[k, :, HEAD_DIM:] = jnp.ones((TOK_DEV, HEAD_DIM), jnp.bfloat16)

    for copy in later:
        copy.wait()


def first_kernel(
    sections, units, later, page, owner, q, keys, values, q_hbm, after,
    o, q_later, bias, spread, sems,
):
    del after
    copies = [pltpu.make_async_copy(region(q_hbm, u), q_later.at[n], sems.at[n]) for n, u in enumerate(later)]
    for copy in copies:
        copy.start()

    @beside
    def _():
        here = lax.axis_index("section")
        prefill_masks(pair_starts(page, here), bias)
        slot_rows(sections, owner, here, spread)
        for n, unit in enumerate(units):
            attend(unit, q.at[n], bias, keys, values, o.at[n])

    for copy in copies:
        copy.wait()


def second_kernel(units, done, q, bias, keys, values, done_o, chip_in, ctx_hbm, o, chip, sems):
    del chip_in, chip
    copies = flushes(done, done_o, ctx_hbm, sems)
    for copy in copies:
        copy.start()

    @beside
    def _():
        for n, unit in enumerate(units):
            attend(unit, q.at[n], bias, keys, values, o.at[n])

    for copy in copies:
        copy.wait()


def unit_cost(units):
    pairs = sum(min(i + 1, REACH + 1) for _, i in units) * GROUP * BLOCK * BLOCK
    return pl.CostEstimate(
        flops=pairs * HEAD_DIM * 8, bytes_accessed=len(units) * BLOCK * GROUP * HEAD_DIM * 4, transcendentals=pairs
    )


def block_shape(units):
    return jax.ShapeDtypeStruct((len(units), BLOCK, GROUP * HEAD_DIM), jnp.bfloat16)


def make_tables(units, page_pair, owner, kv_pool, prefill_q, after, sections):
    kv_local = kv_pool.shape[2] // HEAD_DIM
    return pl.pallas_call(
        functools.partial(tables_kernel, sections, units),
        out_shape=[
            jax.ShapeDtypeStruct(page_pair.shape, jnp.int32),
            jax.ShapeDtypeStruct(owner.shape, jnp.int32),
            jax.ShapeDtypeStruct((kv_local, HEAD_DIM, TOK_DEV), jnp.bfloat16),
            jax.ShapeDtypeStruct((kv_local, TOK_DEV, 2 * HEAD_DIM), jnp.bfloat16),
            jax.ShapeDtypeStruct((ROWS, TOK_DEV), jnp.float32),
            jax.ShapeDtypeStruct((ROWS, sections * CAP * STEPS), jnp.bfloat16),
            block_shape(units),
        ],
        in_specs=[ANY_SPEC] * 5,
        out_specs=[VMEM_SPEC] * 7,
        scratch_shapes=[
            pltpu.VMEM(kv_pool.shape, jnp.bfloat16),
            pltpu.SemaphoreType.DMA((3,)),
            pltpu.SemaphoreType.DMA((len(units),)),
        ],
        compiler_params=params(),
        cost_estimate=unit_cost(units),
        name="make_tables",
    )(in_hbm(page_pair), in_hbm(owner), in_hbm(kv_pool), in_hbm(prefill_q), after)


def prefill_first(units, later, page, owner, q, keys, values, prefill_q, after, sections):
    return pl.pallas_call(
        functools.partial(first_kernel, sections, units, later),
        out_shape=[
            block_shape(units),
            block_shape(later),
            jax.ShapeDtypeStruct((TOK_DEV // BLOCK, BLOCK, LATEST), jnp.float32),
            jax.ShapeDtypeStruct((sections * DSLOT * STEPS, sections * ROWS), jnp.bfloat16),
        ],
        in_specs=[VMEM_SPEC] * 5 + [ANY_SPEC] * 2,
        out_specs=[VMEM_SPEC] * 4,
        scratch_shapes=[pltpu.SemaphoreType.DMA((len(later),))],
        compiler_params=params(),
        cost_estimate=unit_cost(units),
        name="prefill_first",
    )(page, owner, q, keys, values, in_hbm(prefill_q), after)


def prefill_second(units, done, q, bias, keys, values, done_o, ctx_shape, chip):
    return pl.pallas_call(
        functools.partial(second_kernel, units, done),
        out_shape=[ctx_shape, block_shape(units), jax.ShapeDtypeStruct(chip.shape, chip.dtype)],
        in_specs=[VMEM_SPEC] * 6,
        out_specs=[ANY_SPEC, VMEM_SPEC, VMEM_SPEC],
        scratch_shapes=[pltpu.SemaphoreType.DMA((len(done),))],
        input_output_aliases={5: 2},
        compiler_params=params(),
        cost_estimate=unit_cost(units),
        name="prefill_second",
    )(q, bias, keys, values, done_o, chip)


def split_units(kv_local):
    units = [(k, i) for k in range(kv_local) for i in range(TOK_DEV // BLOCK)]
    return units[: len(units) // 2], units[len(units) // 2 :]


def decode_kernel(sections, seen, pick, keys, values, *refs):
    got, (ctx_ref, rows) = refs[:sections], refs[sections:]
    kv_local = keys.shape[0]
    width = kv_local * GROUP * HEAD_DIM
    for k in range(sections):
        for r in range(CAP):
            at = (k * CAP + r) * STEPS
            rows[at : at + STEPS, :] = got[k][r].astype(jnp.float32)
    all_rows = jnp.dot(pick[...], rows[...].astype(jnp.bfloat16), preferred_element_type=jnp.float32)
    all_rows = all_rows.astype(jnp.bfloat16)

    many = GROUP * ROWS
    new_row = lax.broadcasted_iota(jnp.int32, (many, ROWS), 0) % ROWS
    new_col = lax.broadcasted_iota(jnp.int32, (many, ROWS), 1)
    new_allowed = (new_row // STEPS == new_col // STEPS) & (new_col <= new_row)
    contract = (((1,), (1,)), ((), ()))
    for k in range(kv_local):
        q = jnp.concatenate(
            [all_rows[:, (k * GROUP + g) * HEAD_DIM : (k * GROUP + g + 1) * HEAD_DIM] for g in range(GROUP)], axis=0
        )
        new_keys = all_rows[:, width + k * HEAD_DIM : width + (k + 1) * HEAD_DIM]
        at = width + (kv_local + k) * HEAD_DIM
        new_values = all_rows[:, at : at + HEAD_DIM]
        s = jnp.dot(q, keys[k], preferred_element_type=jnp.float32)
        s = (s.reshape(GROUP, ROWS, TOK_DEV) + seen[...][None]).reshape(many, TOK_DEV)
        s_new = lax.dot_general(q, new_keys, contract, preferred_element_type=jnp.float32)
        s_new = jnp.where(new_allowed, s_new, MASKED)
        m_old = jnp.max(s, axis=1, keepdims=True)
        m_new = jnp.max(s_new, axis=1, keepdims=True)
        m = jnp.maximum(m_old, m_new)
        scale_old = jnp.exp2((m_old - m) * EXP2_SCALE)
        scale_new = jnp.exp2((m_new - m) * EXP2_SCALE)
        p = jnp.exp2((s - m_old) * EXP2_SCALE)
        p_new = jnp.exp2((s_new - m_new) * EXP2_SCALE)
        o = jnp.dot(p.astype(jnp.bfloat16), values[k], preferred_element_type=jnp.float32) * scale_old
        total = o[:, HEAD_DIM:] + jnp.sum(p_new, axis=1, keepdims=True) * scale_new
        y = jnp.dot(p_new.astype(jnp.bfloat16), new_values, preferred_element_type=jnp.float32)
        o = o[:, :HEAD_DIM] + y * scale_new
        o = (o / total).astype(jnp.bfloat16)
        for g in range(GROUP):
            ctx_ref[:, (k * GROUP + g) * HEAD_DIM : (k * GROUP + g + 1) * HEAD_DIM] = o[g * ROWS : (g + 1) * ROWS]


def decode(seen, pick, keys, values, got, sections):
    block = got[0].shape
    width = keys.shape[0] * GROUP * HEAD_DIM
    return pl.pallas_call(
        functools.partial(decode_kernel, sections),
        out_shape=jax.ShapeDtypeStruct((ROWS, width), jnp.bfloat16),
        in_specs=[VMEM_SPEC] * (4 + sections),
        out_specs=VMEM_SPEC,
        scratch_shapes=[pltpu.VMEM((sections * CAP * STEPS, block[2]), jnp.float32)],
        compiler_params=params(),
        name="decode_attention",
    )(seen, pick, keys, values, *got)


def project_kernel(sections, flip, *refs):
    ctxs, wo, out_ref = refs[:sections][::-1], refs[sections], refs[-1]
    x = jnp.concatenate([c[...] for c in ctxs], axis=0)
    rows = x.shape[0]
    if rows < BLOCK:
        x = jnp.concatenate([x] * (BLOCK // rows), axis=0)
    out_ref[...] = jnp.dot(x, half_columns(wo, flip)[...], preferred_element_type=jnp.float32)[:rows].astype(out_ref.dtype)


def project(flip, ctxs, wo, after, sections, dtype):
    rows = sections * ROWS
    depth, wide = wo.shape[0], wo.shape[1] // 2
    return pl.pallas_call(
        functools.partial(project_kernel, sections, flip),
        out_shape=jax.ShapeDtypeStruct((rows, wide), dtype),
        in_specs=[VMEM_SPEC] * (sections + 1) + [ANY_SPEC] * len(after),
        out_specs=VMEM_SPEC,
        compiler_params=params(),
        cost_estimate=pl.CostEstimate(flops=rows * depth * wide * 2, bytes_accessed=depth * wide * 2, transcendentals=0),
        name="project_half",
    )(*ctxs[::-1], wo, *after)


def spread_rows(flip, spread, rows, held, out_hbm, sem):
    y = jnp.dot(spread[...], rows[...], preferred_element_type=jnp.float32)
    for slot in range(held.shape[0]):
        held[slot] = y[slot * STEPS : (slot + 1) * STEPS].astype(held.dtype)
    copy = pltpu.make_async_copy(held, half_columns(out_hbm, flip), sem)
    copy.start()
    copy.wait()


def spread_own_kernel(done, spread, rows, done_o, ctx_in, out_hbm, ctx_hbm, held, sem, sems):
    del ctx_in
    copies = flushes(done, done_o, ctx_hbm, sems)
    for copy in copies:
        copy.start()
    spread_rows(False, spread, rows, held, out_hbm, sem)
    for copy in copies:
        copy.wait()


def spread_own(done, spread, rows, done_o, ctx, sections):
    shape = (sections * DSLOT, STEPS, rows.shape[1])
    return pl.pallas_call(
        functools.partial(spread_own_kernel, done),
        out_shape=[
            jax.ShapeDtypeStruct(shape[:2] + (2 * shape[2],), jnp.bfloat16),
            jax.ShapeDtypeStruct(ctx.shape, ctx.dtype),
        ],
        in_specs=[VMEM_SPEC] * 3 + [ANY_SPEC],
        out_specs=[ANY_SPEC] * 2,
        scratch_shapes=[
            pltpu.VMEM(shape, jnp.bfloat16),
            pltpu.SemaphoreType.DMA,
            pltpu.SemaphoreType.DMA((len(done),)),
        ],
        input_output_aliases={3: 1},
        compiler_params=params(),
        name="spread_own",
    )(spread, rows, done_o, ctx)


def spread_other_kernel(spread, rows, out_in, out_hbm, held, sem):
    del out_in
    spread_rows(True, spread, rows, held, out_hbm, sem)


def spread_other(spread, rows, out):
    shape = out.shape[:2] + (rows.shape[1],)
    return pl.pallas_call(
        spread_other_kernel,
        out_shape=jax.ShapeDtypeStruct(out.shape, out.dtype),
        in_specs=[VMEM_SPEC] * 2 + [ANY_SPEC],
        out_specs=ANY_SPEC,
        scratch_shapes=[pltpu.VMEM(shape, jnp.bfloat16), pltpu.SemaphoreType.DMA],
        input_output_aliases={2: 0},
        compiler_params=params(),
        name="spread_other",
    )(spread, rows, out)


def swap(x, axis, k):
    count = lax.axis_size(axis)
    return lax.ppermute(x, axis, [(i, i ^ k) for i in range(count)])


def per_device(prefill_q, kv_pool, decode_q, decode_kv, wo_weight, page_pair, slot_owner):
    sections = lax.axis_size("section")
    owner = slot_owner.reshape(-1)
    units = split_units(kv_pool.shape[2] // HEAD_DIM)
    ctx_shape = jax.ShapeDtypeStruct(prefill_q.shape, prefill_q.dtype)

    packed = pack(owner, decode_q, decode_kv, sections)
    first, second = routes(FIRST_ROUND, sections), routes(SECOND_ROUND, sections)
    got = [packed[0]] + [send(x, route) for x, route in zip(packed[1:], first[1:])]
    page, owner, keys, values, seen, pick, q = make_tables(
        units[0], page_pair, owner.reshape(1, -1), kv_pool, prefill_q, packed[0], sections
    )
    ctx = decode(seen, pick, keys, values, got, sections)
    ctxs = [ctx] + [send(ctx, route) for route in second[1:]]
    done_o, q, bias, spread = prefill_first(
        units[0], units[1], page, owner, q, keys, values, prefill_q, ctx, sections
    )

    away = project(True, ctxs, wo_weight, [q], sections, jnp.bfloat16)
    came = swap(away, "tensor", 1)
    keep = project(False, ctxs, wo_weight, [], sections, jnp.float32)
    chip = keep + came.astype(jnp.float32)
    k = 2
    while k < lax.axis_size("tensor"):
        far = swap(chip.astype(jnp.bfloat16), "tensor", k)
        if k == 2:
            prefill_ctx, done_o, chip = prefill_second(
                units[1], units[0], q, bias, keys, values, done_o, ctx_shape, chip
            )
        chip = chip + far.astype(jnp.float32)
        k *= 2
    mine = chip.astype(jnp.bfloat16)
    other = swap(mine, "tensor", 1)
    decode_out, prefill_ctx = spread_own(units[1], spread, mine, done_o, prefill_ctx, sections)
    decode_out = spread_other(spread, other, decode_out)
    return (prefill_ctx, decode_out)


def solution(mesh):
    placed = (
        P(("groups", "section"), "tensor"),
        P(None, ("groups", "section"), "tensor"),
        P(("groups", "section"), None, "tensor"),
        P(None, ("groups", "section"), None, "tensor"),
        P("tensor", "section"),
        P("groups", None),
        P("groups", None),
    )
    return jax.shard_map(
        per_device,
        mesh=mesh,
        in_specs=placed,
        out_specs=(P(("groups", "section"), "tensor"), P("groups", None, "section")),
        check_vma=False,
    )
```
